512 devices in a mesh: rad: 32 (over z, y_hi), azi: 16 (over y_lo, x, core).
Axes of the slice: x: 4, y: 8 (y_hi: 4, y_lo: 2; y = y_hi * 2 + y_lo), z: 8, core: 2. Of those that a mesh axis runs over, the one named last changes fastest.
Arguments:
- density: float32 [512, 2048, 128], P('rad', 'azi'), may hold values from -6 to 6
Outputs:
- potential: float32 [512, 2048, 128], P('rad', 'azi')
The draws below stay inside these ranges and needn't reach their ends.
All inputs are finite; a program needn't handle non-finite values.
Results may differ from the reference program's by a relative error of at most 0.000073.
Values sent between devices are 32-bit elements; how exact they have to be, the bound alone decides.
No kernel may reach another device: no remote copies, remote signals or barrier semaphores. Data moves between devices by JAX's collectives and lax.ppermute only.
A program may use at most 64 MiB of HBM per device.

```python
import math
import jax
import jax.numpy as jnp
from jax import lax

NPHI = 2048
MODES = 256
NZ = 128
SWEEPS = 4
NR = 512


def levels(own_key, extent, shards, smallest, high):
    level = 1.0
    for axis_at, blocks in shards:
        steps = jax.random.uniform(jax.random.fold_in(jax.random.fold_in(own_key, 6), axis_at), (blocks,), jnp.float32, smallest / len(shards), high / len(shards))
        level = level * jnp.repeat(jnp.exp(steps), extent[axis_at] // blocks).reshape((-1,) + (1,) * (len(extent) - 1 - axis_at))
    return level


def scatter_about(rng, shape, spread, limit, cuts=(), held_as=jnp.bfloat16):
    values = jax.random.normal(rng, shape, jnp.float32) * spread
    if len(cuts) > 0:
        values = levels(rng, shape, cuts, -0.22, 0.18) * values
    return jnp.clip(values, min=-limit, max=limit).astype(held_as)


def setup_inputs(seed: int = 0) -> dict:
    seeds = jax.random.split(jax.random.key(seed), 2)
    density = scatter_about(seeds[0], (NR, NPHI, NZ), 1.0, 6.0, ((0, 32), (1, 16)), jnp.float32)
    return {"density": density}


low_bound = 0.1
high_bound = 2.0
theta = 0.5 * (high_bound + low_bound)
delta = 0.5 * (high_bound - low_bound)
sigma = theta / delta
four_pi = 4.0 * math.pi


def basis(mode_first, mode_count, phi_first, phi_count, length, forward):
    modes = mode_first + jnp.arange(mode_count, dtype=jnp.int32)
    cells = phi_first + jnp.arange(phi_count, dtype=jnp.int32)
    product = (cells[:, None] * modes[None, :]) % length
    angle = product.astype(jnp.float32) * (2.0 * math.pi / length)
    if forward:
        weight = jnp.full((mode_count,), 1.0 / length, jnp.float32)
    else:
        weight = jnp.where(modes == 0, 1.0, 2.0).astype(jnp.float32)
    table = jnp.stack([jnp.cos(angle) * weight, jnp.sin(angle) * weight], axis=2)
    return table.reshape(phi_count, 2 * mode_count)


def solve(source, mode_first, radius_first, extend):
    count, _, rows, depth = source.shape
    modes = (mode_first + jnp.arange(count, dtype=jnp.int32)).astype(jnp.float32)
    radius = (radius_first + jnp.arange(rows, dtype=jnp.int32)).astype(jnp.float32) + 0.5
    diagonal = (4.0 + (modes[:, None] * modes[:, None]) / (radius[None, :] * radius[None, :])).reshape(count, 1, rows, 1)
    outer_weight = (1.0 + 0.5 / radius).reshape(1, 1, rows, 1)
    inner_weight = (1.0 - 0.5 / radius).reshape(1, 1, rows, 1)
    ratio = 1.0 / sigma
    update = source / diagonal / theta
    iterate = update
    for sweep in range(SWEEPS - 1):
        padded = extend(iterate)
        vertical = jnp.pad(iterate, ((0, 0), (0, 0), (0, 0), (1, 1)))
        image = diagonal * iterate - outer_weight * padded[:, :, 2:, :] - inner_weight * padded[:, :, :-2, :]
        image = image - vertical[:, :, :, 2:] - vertical[:, :, :, :-2]
        residual = source - image
        next_ratio = 1.0 / (2.0 * sigma - ratio)
        update = (next_ratio * ratio) * update + (2.0 * next_ratio / delta) * (residual / diagonal)
        iterate = iterate + update
        ratio = next_ratio
    return iterate


def pad_radial(field):
    return jnp.pad(field, ((0, 0), (0, 0), (1, 1), (0, 0)))


def reference(density):
    forward_table = basis(0, MODES, 0, NPHI, NPHI, True)
    spectrum = jnp.einsum("rjz,jk->krz", density, forward_table, precision=lax.Precision.HIGHEST)
    spectrum = spectrum.reshape(MODES, 2, NR, NZ)
    solved = solve(-four_pi * spectrum, 0, 0, pad_radial)
    inverse_table = basis(0, MODES, 0, NPHI, NPHI, False)
    return jnp.einsum("krz,jk->rjz", solved.reshape(2 * MODES, NR, NZ), inverse_table, precision=lax.Precision.HIGHEST)
```

```python
import functools
import math

import jax
import jax.numpy as jnp
import numpy as np
from jax import lax
from jax.experimental import pallas as pl
from jax.experimental.pallas import tpu as pltpu
from jax.sharding import PartitionSpec as P

NPHI = 2048
MODES = 256
SWEEPS = 4
SECTORS = 16
SECTOR = NPHI // SECTORS
COEFS = 2 * MODES
RANK = 48
ROWS = 16
DEPTH = 128
GROUP = 8
LANES = 128

low_bound = 0.1
high_bound = 2.0
theta = 0.5 * (high_bound + low_bound)
delta = 0.5 * (high_bound - low_bound)
sigma = theta / delta
four_pi = 4.0 * math.pi

BF = jnp.bfloat16
F32 = jnp.float32


def split_table(table):
    high = table.astype(np.float32).astype(BF)
    low = (table - high.astype(np.float64)).astype(np.float32).astype(BF)
    return high, low


@functools.cache
def tables():
    modes = np.arange(MODES)
    angle = 2.0 * np.pi * ((np.arange(SECTOR)[:, None] * modes[None, :]) % NPHI) / NPHI
    first = np.concatenate([np.cos(angle), np.sin(angle)], axis=1)
    left, _, _ = np.linalg.svd(first, full_matrices=False)
    left = left[:, :RANK]
    cores = []
    for sector in range(SECTORS):
        cells = sector * SECTOR + np.arange(SECTOR)
        angle = 2.0 * np.pi * ((cells[:, None] * modes[None, :]) % NPHI) / NPHI
        cores.append(left.T @ np.concatenate([np.cos(angle), np.sin(angle)], axis=1))
    core = np.concatenate(cores, axis=0)
    weight = np.where(np.tile(modes, 2) == 0, 1.0, 2.0)
    left_high, left_low = split_table(left)
    forward = split_table(core.T * (-four_pi / NPHI))
    inverse = split_table(core * weight[None, :])
    squeeze = np.concatenate(
        [
            np.concatenate([left_high.T, left_high.T], axis=1),
            np.concatenate([left_low.T, left_low.T], axis=1),
        ],
        axis=0,
    )
    stretch = np.concatenate([left_high, left_high, left_low, left_low], axis=1)
    return squeeze, forward, inverse, stretch


def halves(value):
    high = value.astype(BF)
    low = (value - high.astype(F32)).astype(BF)
    return high, low


def dot(a, b):
    return jnp.dot(a, b, preferred_element_type=F32)


def lane_group(shape):
    return lax.broadcasted_iota(jnp.int32, shape, 1) // GROUP


def swap_groups(blocks):
    blocks = list(blocks)
    group = lane_group(blocks[0].shape)
    for bit in (1, 2, 4, 8):
        keep = (group & bit) == 0
        for i in range(16):
            if i & bit:
                continue
            j = i | bit
            one, two = blocks[i], blocks[j]
            blocks[i] = jnp.where(keep, one, pltpu.roll(two, GROUP * bit, 1))
            blocks[j] = jnp.where(keep, pltpu.roll(one, LANES - GROUP * bit, 1), two)
    return blocks


def compress_kernel(x_ref, squeeze_ref, out_ref, y_ref):
    squeeze = squeeze_ref[...]
    for r in range(0, ROWS, 2):
        columns = []
        for k in range(2):
            columns.append(jnp.concatenate(halves(x_ref[r + k]), axis=0))
        y = dot(squeeze, jnp.concatenate(columns, axis=1))
        y = y[:RANK] + y[RANK:]
        y_ref[r] = y[:, :LANES]
        y_ref[r + 1] = y[:, LANES:]
    inside = lax.broadcasted_iota(jnp.int32, (8, LANES), 1) % GROUP
    for c in range(0, RANK, 8):
        rows = [pltpu.roll(y_ref[r, c : c + 8, :], 4, 1) for r in range(ROWS)]
        groups = swap_groups(rows)
        edge = groups[0]
        groups[0] = jnp.where(inside >= 4, edge, 0.0)
        groups.append(jnp.where(inside < 4, edge, 0.0))
        for q in range(SECTORS):
            out_ref[q, c : c + 8, :LANES] = groups[q]
            out_ref[q, c : c + 8, LANES:] = groups[q + 1]


def source_kernel(p_ref, high_ref, low_ref, s_ref, down_ref, up_ref):
    p_high, p_low = halves(p_ref[...])
    step = 128
    for m in range(0, COEFS, step):
        w_high = high_ref[m : m + step, :]
        w_low = low_ref[m : m + step, :]
        s_ref[m : m + step, :] = dot(w_high, p_high) + dot(w_high, p_low) + dot(w_low, p_high)
    lane = lax.broadcasted_iota(jnp.int32, (8, LANES), 1)
    for m in range(0, MODES, 8):
        pieces = [
            s_ref[half + m : half + m + 8, h : h + LANES]
            for half in (0, MODES)
            for h in (0, LANES)
        ]
        down = pieces[0]
        up = pltpu.roll(pieces[0], 24, 1)
        for k in (1, 2, 3):
            down = jnp.where(lane < 24 * k, down, pltpu.roll(pieces[k], 24 * k, 1))
            up = jnp.where(lane < 24 * k, up, pltpu.roll(pieces[k], 24 * k + 24, 1))
        down_ref[m : m + 8, :] = down
        up_ref[m : m + 8, :] = up


def solve_kernel(place_ref, s_ref, low_ref, high_ref, vh_ref, vl_ref, out_ref, own_ref):
    shape = (8, LANES)
    lane = lax.broadcasted_iota(jnp.int32, shape, 1)
    slot = lane // GROUP
    inside = lane % GROUP
    row_first = place_ref[0]
    row_count = place_ref[1]
    depth_first = place_ref[2]
    main_row = slot + row_first
    halo_row = jnp.where(slot < 8, slot + 16, slot - 16) + row_first
    depths = [depth_first - 4 + h * GROUP + inside for h in range(2)]
    last, first = slot == 15, slot == 0

    def weights(row):
        radius = row.astype(F32) + 0.5
        inverse = 1.0 / radius
        return 1.0 + 0.5 * inverse, 1.0 - 0.5 * inverse, inverse * inverse

    main_out, main_in, main_square = weights(main_row)
    halo_out, halo_in, halo_square = weights(halo_row)

    def valid(row, depth):
        good = (row >= 0) & (row < row_count) & (depth >= 0) & (depth < DEPTH)
        return jnp.where(good, 1.0, 0.0).astype(F32)

    main_valid = [valid(main_row, d) for d in depths]
    halo_valid = [valid(halo_row, d) for d in depths]

    def turn(value, amount):
        return pltpu.roll(value, amount % LANES, 1)

    def vertical(pair):
        lower, upper = pair
        return [
            jnp.where(inside == 7, turn(upper, 7), turn(lower, -1)) + turn(lower, 1),
            turn(upper, -1) + jnp.where(inside == 0, turn(lower, -7), turn(upper, 1)),
        ]

    ratios = []
    ratio = 1.0 / sigma
    for _ in range(SWEEPS - 1):
        following = 1.0 / (2.0 * sigma - ratio)
        ratios.append((following * ratio, 2.0 * following / delta))
        ratio = following

    @pl.loop(0, MODES // 8, unroll=2)
    def _(group):
        m = pl.multiple_of(group * 8, 8)
        mode = (lax.broadcasted_iota(jnp.int32, shape, 0) + m).astype(F32)
        square = mode * mode
        main_inv = 1.0 / (4.0 + square * main_square)
        halo_inv = 1.0 / (4.0 + square * halo_square)
        main_invs = [main_inv * v for v in main_valid]
        halo_invs = [halo_inv * v for v in halo_valid]
        low = low_ref[pl.ds(m, 8), :]
        high = high_ref[pl.ds(m, 8), :]
        for part in range(2):
            at = pl.multiple_of(part * MODES + m, 8)
            main_s = [s_ref[pl.ds(at, 8), h * LANES : (h + 1) * LANES] for h in range(2)]
            halo_s = []
            for h in range(2):
                k = 2 * part + h
                after = turn(high, -24 * k)
                before = turn(low, 104 - 24 * k)
                halo_s.append(
                    jnp.where(slot < 3, after, jnp.where(slot >= 13, before, 0.0))
                )
            main_u = [s * i * (1.0 / theta) for s, i in zip(main_s, main_invs)]
            halo_u = [s * i * (1.0 / theta) for s, i in zip(halo_s, halo_invs)]
            main, halo = list(main_u), list(halo_u)
            for sweep in range(SWEEPS - 1):
                keep, push = ratios[sweep]
                ends = sweep == SWEEPS - 2
                main_z = vertical(main)
                halo_z = None if ends else vertical(halo)
                for h in range(2):
                    main_next, main_prev = turn(main[h], -8), turn(main[h], 8)
                    halo_next, halo_prev = turn(halo[h], -8), turn(halo[h], 8)
                    total = main_s[h] + main_z[h]
                    total = total + main_out * jnp.where(last, halo_next, main_next)
                    total = total + main_in * jnp.where(first, halo_prev, main_prev)
                    main_u[h] = keep * main_u[h] + push * (total * main_invs[h] - main[h])
                    if not ends:
                        total = halo_s[h] + halo_z[h]
                        total = total + halo_out * jnp.where(last, main_next, halo_next)
                        total = total + halo_in * jnp.where(first, main_prev, halo_prev)
                        halo_u[h] = keep * halo_u[h] + push * (total * halo_invs[h] - halo[h])
                for h in range(2):
                    main[h] = main[h] + main_u[h]
                    if not ends:
                        halo[h] = halo[h] + halo_u[h]
            own_ref[pl.ds(at, 8), :] = jnp.where(inside < 4, turn(main[0], -4), turn(main[1], 4))

    own_high, own_low = halves(own_ref[...])
    both = jnp.concatenate([own_high, own_low], axis=1)
    step = 96
    for m in range(0, SECTORS * RANK, step):
        wide = dot(vh_ref[m : m + step, :], both)
        out_ref[m : m + step, :] = (
            wide[:, :LANES] + wide[:, LANES:] + dot(vl_ref[m : m + step, :], own_high)
        )


def expand_kernel(q_ref, stretch_ref, out_ref, y_ref):
    for c in range(0, RANK, 8):
        rows = swap_groups([q_ref[q, c : c + 8, :] for q in range(SECTORS)])
        for r in range(ROWS):
            y_ref[r, c : c + 8, :] = rows[r]
    stretch = stretch_ref[...]
    for r in range(0, ROWS, 2):
        columns = []
        for k in range(2):
            high, low = halves(y_ref[r + k])
            columns.append(jnp.concatenate([high, low, high, low], axis=0))
        wide = dot(stretch, jnp.concatenate(columns, axis=1))
        out_ref[r] = wide[:, :LANES]
        out_ref[r + 1] = wide[:, LANES:]


def call(kernel, outs, scratch, name, first_in_smem=False, count=1, **options):
    whole = pl.BlockSpec(memory_space=pltpu.VMEM)
    specs = [whole] * count
    if first_in_smem:
        specs[0] = pl.BlockSpec(memory_space=pltpu.SMEM)
    single = len(outs) == 1
    shapes = [jax.ShapeDtypeStruct(shape, F32) for shape in outs]
    return pl.pallas_call(
        kernel,
        out_shape=shapes[0] if single else shapes,
        in_specs=specs,
        out_specs=whole if single else [whole] * len(outs),
        scratch_shapes=[pltpu.VMEM(shape, F32) for shape in scratch],
        compiler_params=pltpu.CompilerParams(vmem_limit_bytes=40 * 1024 * 1024),
        name=name,
        **options,
    )


def compress(density, squeeze, **options):
    return call(
        compress_kernel,
        [(SECTORS, RANK, 2 * LANES)],
        [(ROWS, RANK, LANES)],
        "compress",
        count=2,
        **options,
    )(density, squeeze)


def make_source(received, high, low, **options):
    return call(
        source_kernel,
        [(COEFS, 2 * LANES), (MODES, LANES), (MODES, LANES)],
        [],
        "make_source",
        count=3,
        **options,
    )(received, high, low)


def solve(place, source, low, high, v_high, v_low, **options):
    return call(
        solve_kernel,
        [(SECTORS * RANK, LANES)],
        [(COEFS, LANES)],
        "solve",
        first_in_smem=True,
        count=6,
        **options,
    )(place, source, low, high, v_high, v_low)


def expand(received, stretch, **options):
    return call(
        expand_kernel,
        [(ROWS, SECTOR, DEPTH)],
        [(ROWS, RANK, LANES)],
        "expand",
        count=2,
        **options,
    )(received, stretch)


def per_device(density):
    squeeze, forward, inverse, stretch = (
        jax.tree.map(jnp.asarray, item) for item in tables()
    )
    count = lax.axis_size("rad")
    place = jnp.stack(
        [
            lax.axis_index("rad") * ROWS,
            jnp.int32(count * ROWS),
            lax.axis_index("azi") * GROUP,
        ]
    ).astype(jnp.int32)
    outgoing = compress(density, squeeze)
    received = lax.all_to_all(outgoing, "azi", 0, 0)
    received = received.reshape(SECTORS * RANK, 2 * LANES)
    source, down, up = make_source(received, *forward)
    low = lax.ppermute(up, "rad", [(i, i + 1) for i in range(count - 1)])
    high = lax.ppermute(down, "rad", [(i + 1, i) for i in range(count - 1)])
    solved = solve(place, source, low, high, *inverse)
    received = lax.all_to_all(solved.reshape(SECTORS, RANK, LANES), "azi", 0, 0)
    return expand(received, stretch)


def solution(mesh):
    spec = P("rad", "azi", None)
    return jax.shard_map(
        per_device, mesh=mesh, in_specs=(spec,), out_specs=spec, check_vma=False
    )
```

```python
import functools
import math

import jax
import jax.numpy as jnp
import numpy as np
from jax import lax
from jax.experimental import pallas as pl
from jax.experimental.pallas import tpu as pltpu
from jax.sharding import PartitionSpec as P

NPHI = 2048
MODES = 256
SWEEPS = 4
SECTORS = 16
SECTOR = NPHI // SECTORS
COEFS = 2 * MODES
RANK = 48
ROWS = 16
DEPTH = 128
GROUP = 8
LANES = 128
HALF = RANK // 2
BLOCKS = 8
BLOCK_ROWS = 8
EXTENDED = BLOCK_ROWS + 6
CELLS = 3 * GROUP * BLOCK_ROWS
CHUNKS = 4

low_bound = 0.1
high_bound = 2.0
theta = 0.5 * (high_bound + low_bound)
delta = 0.5 * (high_bound - low_bound)
sigma = theta / delta
four_pi = 4.0 * math.pi

BF = jnp.bfloat16
F32 = jnp.float32


def split_table(table):
    high = table.astype(np.float32).astype(BF)
    low = (table - high.astype(np.float64)).astype(np.float32).astype(BF)
    return high, low


@functools.cache
def tables():
    modes = np.arange(MODES)
    angle = 2.0 * np.pi * ((np.arange(SECTOR)[:, None] * modes[None, :]) % NPHI) / NPHI
    first = np.concatenate([np.cos(angle), np.sin(angle)], axis=1)
    left, _, _ = np.linalg.svd(first, full_matrices=False)
    left = left[:, :RANK]
    cores = []
    for sector in range(SECTORS):
        cells = sector * SECTOR + np.arange(SECTOR)
        angle = 2.0 * np.pi * ((cells[:, None] * modes[None, :]) % NPHI) / NPHI
        cores.append(left.T @ np.concatenate([np.cos(angle), np.sin(angle)], axis=1))
    core = np.concatenate(cores, axis=0)
    weight = np.where(np.tile(modes, 2) == 0, 1.0, 2.0)
    left_high, left_low = split_table(left)
    ordered = core.reshape(SECTORS, 2, HALF, COEFS).transpose(1, 0, 2, 3)
    forward = split_table(ordered.reshape(SECTORS * RANK, COEFS) * (-four_pi / NPHI))
    inverse = split_table(core * weight[None, :])
    squeeze = np.concatenate(
        [
            np.concatenate([left_high.T, left_high.T], axis=1),
            np.concatenate([left_low.T, left_low.T], axis=1),
        ],
        axis=0,
    )
    stretch = np.concatenate([left_high, left_high, left_low, left_low], axis=1)
    return squeeze, forward, inverse, stretch


def halves(value):
    high = value.astype(BF)
    low = (value - high.astype(F32)).astype(BF)
    return high, low


def dot(a, b):
    return jnp.dot(a, b, preferred_element_type=F32)


def swap_groups(blocks, size):
    blocks = list(blocks)
    group = lax.broadcasted_iota(jnp.int32, blocks[0].shape, 1) // size
    bit = 1
    while bit < len(blocks):
        keep = (group & bit) == 0
        for i in range(len(blocks)):
            if i & bit:
                continue
            j = i | bit
            one, two = blocks[i], blocks[j]
            blocks[i] = jnp.where(keep, one, pltpu.roll(two, size * bit, 1))
            blocks[j] = jnp.where(keep, pltpu.roll(one, LANES - size * bit, 1), two)
        bit *= 2
    return blocks


def compress_kernel(x_hbm, squeeze_hbm, out_ref, x_ref, squeeze_ref, y_ref, sems):
    table_copy = pltpu.make_async_copy(squeeze_hbm, squeeze_ref, sems.at[CHUNKS])
    table_copy.start()
    rows = ROWS // CHUNKS
    copies = []
    for k in range(CHUNKS):
        part = pl.ds(k * rows, rows)
        copies.append(pltpu.make_async_copy(x_hbm.at[part], x_ref.at[part], sems.at[k]))
        copies[-1].start()
    table_copy.wait()
    squeeze = squeeze_ref[...]
    for r in range(0, ROWS, 2):
        if r % rows == 0:
            copies[r // rows].wait()
        columns = []
        for k in range(2):
            columns.append(jnp.concatenate(halves(x_ref[r + k]), axis=0))
        y = dot(squeeze, jnp.concatenate(columns, axis=1))
        y = y[:RANK] + y[RANK:]
        y_ref[r] = y[:, :LANES]
        y_ref[r + 1] = y[:, LANES:]
    lane = lax.broadcasted_iota(jnp.int32, (8, LANES), 1)
    inside = lane % GROUP
    for c in range(0, HALF, 8):
        pair = []
        for start in (c, c + HALF):
            groups = swap_groups(
                [pltpu.roll(y_ref[r, start : start + 8, :], 4, 1) for r in range(ROWS)], GROUP
            )
            edge = groups[0]
            groups[0] = jnp.where(inside >= 4, edge, 0.0)
            groups.append(jnp.where(inside < 4, edge, 0.0))
            pair.append(groups)
        for g in range(2 * BLOCKS + 1):
            one, two = pair[0][g], pair[1][g]
            packed = (
                jnp.where(lane < 64, one, pltpu.roll(two, 64, 1)),
                jnp.where(lane < 64, pltpu.roll(one, 64, 1), two),
            )
            for j in range(3):
                if (g - j) % 2 or not 0 <= (g - j) // 2 < BLOCKS:
                    continue
                for side in range(2):
                    at = j * HALF + c
                    out_ref[g - j + side, at : at + 8, :] = packed[side]


def source_kernel(p_ref, high_ref, low_ref, s_ref, down_ref, up_ref):
    turned = []
    for j in range(3):
        block = p_ref[:, j * HALF : (j + 1) * HALF, :].reshape(SECTORS * HALF, LANES).T
        turned.append(jnp.concatenate([block[:64], block[64:]], axis=1))
    cells_high, cells_low = halves(jnp.concatenate(turned, axis=0))
    both = jnp.concatenate([cells_high, cells_low], axis=0)
    for n in range(0, COEFS, 256):
        wide = dot(both, high_ref[:, n : n + 256])
        s_ref[:, n : n + 256] = (
            wide[:CELLS] + wide[CELLS:] + dot(cells_high, low_ref[:, n : n + 256])
        )
    level = lax.broadcasted_iota(jnp.int32, (8, COEFS), 0)

    def at(j, r):
        start = j * 64 + r * 8
        return s_ref[start : start + 8, :]

    for ref, (near, middle, far) in ((down_ref, (0, 1, 2)), (up_ref, (7, 6, 5))):
        ref[0:8, :] = jnp.where(level < 4, at(2, far), at(0, far))
        ref[8:16, :] = jnp.where(level < 2, pltpu.roll(at(2, middle), 5, 0), at(0, near))
        ref[16:24, :] = at(2, near)
        ref[24:32, :] = jnp.where(level < 3, at(2, middle), at(0, middle))
        ref[32:40, :] = at(1, near)
        ref[40:48, :] = at(1, middle)
        ref[48:56, :] = at(1, far)


def solve_kernel(
    place_ref, s_ref, low_ref, high_ref, vh_ref, vl_ref, out_ref, inverse_ref, weight_ref, own_ref
):
    shape = (8, LANES)
    level = lax.broadcasted_iota(jnp.int32, shape, 0)
    lane = lax.broadcasted_iota(jnp.int32, shape, 1)
    row_first = place_ref[0]
    row_count = place_ref[1]
    depth_first = place_ref[2]
    bottom = jnp.where(depth_first - 4 + level >= 0, 1.0, 0.0).astype(F32)
    top = jnp.where(depth_first + 12 + level < DEPTH, 1.0, 0.0).astype(F32)

    for e in range(EXTENDED):
        row = jnp.full(shape, row_first + (e - 3), jnp.int32)
        inverse = 1.0 / (row.astype(F32) + 0.5)
        weight_ref[e, 0] = 1.0 + 0.5 * inverse
        weight_ref[e, 1] = 1.0 - 0.5 * inverse
        good = jnp.where((row >= 0) & (row < row_count), 1.0, 0.0).astype(F32)
        for t in range(2):
            ratio = (lane + t * LANES).astype(F32) * inverse
            inverse_ref[t, e] = good / (4.0 + ratio * ratio)

    def turn(value, amount):
        return pltpu.roll(value, amount % 8, 0)

    ratios = []
    ratio = 1.0 / sigma
    for _ in range(SWEEPS - 1):
        following = 1.0 / (2.0 * sigma - ratio)
        ratios.append((following * ratio, 2.0 * following / delta))
        ratio = following

    @pl.loop(0, 4)
    def _(tile):
        lanes = pl.ds(pl.multiple_of(tile * LANES, LANES), LANES)
        table = tile % 2

        def load(ref, start):
            return ref[start : start + 8, lanes]

        def halo(ref, distance):
            if distance == 3:
                both = load(ref, 0)
                return [both, load(ref, 48), both]
            if distance == 2:
                both = load(ref, 24)
                rest = turn(load(ref, 8), 3)
                return [both, load(ref, 40), jnp.where(level < 3, both, rest)]
            return [load(ref, 8), load(ref, 32), load(ref, 16)]

        def source(e):
            if e < 3:
                return halo(low_ref, 3 - e)
            if e >= 11:
                return halo(high_ref, e - 10)
            return [load(s_ref, j * 64 + (e - 3) * 8) for j in range(3)]

        given, scale, step = {}, {}, {}
        state = [{} for _ in range(SWEEPS)]
        for newest in range(EXTENDED + SWEEPS - 1):
            e = newest
            if e < EXTENDED:
                given[e] = source(e)
                middle = inverse_ref[table, e]
                scale[e] = [middle * bottom, middle, middle * top]
                step[e] = [g * i * (1.0 / theta) for g, i in zip(given[e], scale[e])]
                state[0][e] = step[e]
            for sweep in range(1, SWEEPS):
                e = newest - sweep
                if not sweep <= e < EXTENDED - sweep:
                    continue
                keep, push = ratios[sweep - 1]
                old = state[sweep - 1]
                center, outer, inner = old[e], old[e + 1], old[e - 1]
                out_weight, in_weight = weight_ref[e, 0], weight_ref[e, 1]
                above = [turn(x, -1) for x in center]
                below = [turn(x, 1) for x in center]
                steps, values = [], []
                for j in range(3):
                    higher = above[j]
                    if j < 2:
                        higher = jnp.where(level == 7, above[j + 1], higher)
                    lower = below[j]
                    if j > 0:
                        lower = jnp.where(level == 0, below[j - 1], lower)
                    total = given[e][j] + (higher + lower)
                    total = total + (out_weight * outer[j] + in_weight * inner[j])
                    move = keep * step[e][j] + push * (total * scale[e][j] - center[j])
                    steps.append(move)
                    values.append(center[j] + move)
                step[e] = steps
                state[sweep][e] = values
            e = newest - (SWEEPS - 1)
            if 3 <= e < 11:
                x = state[SWEEPS - 1][e]
                at = (e - 3) * 16
                own_ref[at : at + 8, lanes] = turn(jnp.where(level < 4, x[1], x[0]), 4)
                own_ref[at + 8 : at + 16, lanes] = turn(jnp.where(level < 4, x[2], x[1]), 4)

    own_high, own_low = halves(own_ref[...])
    both = jnp.concatenate([own_high, own_low], axis=0)

    def across(a, b):
        return lax.dot_general(a, b, (((1,), (1,)), ((), ())), preferred_element_type=F32)

    step_rows = 192
    for m in range(0, SECTORS * RANK, step_rows):
        wide = across(vh_ref[m : m + step_rows, :], both)
        out_ref[m : m + step_rows, :] = (
            wide[:, :LANES]
            + wide[:, LANES:]
            + across(vl_ref[m : m + step_rows, :], own_high)
        )


def expand_kernel(q_ref, stretch_ref, out_hbm, y_ref, out_ref, sems):
    for side in range(2):
        for c in range(0, RANK, 8):
            rows = swap_groups(
                [q_ref[2 * b + side, c : c + 8, :] for b in range(BLOCKS)], 2 * GROUP
            )
            for r in range(BLOCK_ROWS):
                y_ref[side * BLOCK_ROWS + r, c : c + 8, :] = rows[r]
    stretch = stretch_ref[...]
    rows = ROWS // CHUNKS
    copies = []
    for r in range(0, ROWS, 2):
        columns = []
        for k in range(2):
            high, low = halves(y_ref[r + k])
            columns.append(jnp.concatenate([high, low, high, low], axis=0))
        wide = dot(stretch, jnp.concatenate(columns, axis=1))
        out_ref[r] = wide[:, :LANES]
        out_ref[r + 1] = wide[:, LANES:]
        if (r + 2) % rows == 0:
            part = pl.ds(r + 2 - rows, rows)
            copies.append(
                pltpu.make_async_copy(out_ref.at[part], out_hbm.at[part], sems.at[len(copies)])
            )
            copies[-1].start()
    for copy in copies:
        copy.wait()


VMEM = pl.BlockSpec(memory_space=pltpu.VMEM)
SMEM = pl.BlockSpec(memory_space=pltpu.SMEM)
HBM = pl.BlockSpec(memory_space=pltpu.HBM)


def call(kernel, outs, in_specs, scratch, name, out_space=VMEM, **options):
    single = len(outs) == 1
    shapes = [jax.ShapeDtypeStruct(shape, F32) for shape in outs]
    return pl.pallas_call(
        kernel,
        out_shape=shapes[0] if single else shapes,
        in_specs=in_specs,
        out_specs=out_space if single else [out_space] * len(outs),
        scratch_shapes=scratch,
        compiler_params=pltpu.CompilerParams(vmem_limit_bytes=40 * 1024 * 1024),
        name=name,
        **options,
    )


def compress(density, squeeze, **options):
    return call(
        compress_kernel,
        [(SECTORS, 3 * HALF, LANES)],
        [HBM, HBM],
        [
            pltpu.VMEM((ROWS, SECTOR, DEPTH), F32),
            pltpu.VMEM((2 * RANK, 2 * SECTOR), BF),
            pltpu.VMEM((ROWS, RANK, LANES), F32),
            pltpu.SemaphoreType.DMA((CHUNKS + 1,)),
        ],
        "compress",
        **options,
    )(density, squeeze)


def make_source(received, high, low, **options):
    return call(
        source_kernel,
        [(CELLS, COEFS), (56, COEFS), (56, COEFS)],
        [VMEM] * 3,
        [],
        "make_source",
        **options,
    )(received, high, low)


def solve(place, source, low, high, v_high, v_low, **options):
    return call(
        solve_kernel,
        [(SECTORS * RANK, LANES)],
        [SMEM] + [VMEM] * 5,
        [
            pltpu.VMEM((2, EXTENDED, 8, LANES), F32),
            pltpu.VMEM((EXTENDED, 2, 8, LANES), F32),
            pltpu.VMEM((LANES, COEFS), F32),
        ],
        "solve",
        **options,
    )(place, source, low, high, v_high, v_low)


def expand(received, stretch, **options):
    return call(
        expand_kernel,
        [(ROWS, SECTOR, DEPTH)],
        [VMEM] * 2,
        [
            pltpu.VMEM((ROWS, RANK, LANES), F32),
            pltpu.VMEM((ROWS, SECTOR, DEPTH), F32),
            pltpu.SemaphoreType.DMA((CHUNKS,)),
        ],
        "expand",
        out_space=HBM,
        **options,
    )(received, stretch)


def per_device(density):
    squeeze, forward, inverse, stretch = (
        jax.tree.map(jnp.asarray, item) for item in tables()
    )
    count = lax.axis_size("rad")
    azi = lax.axis_index("azi")
    place = jnp.stack(
        [
            lax.axis_index("rad") * ROWS + azi % 2 * BLOCK_ROWS,
            jnp.int32(count * ROWS),
            azi // 2 * 2 * GROUP,
        ]
    ).astype(jnp.int32)
    outgoing = compress(density, squeeze)
    received = lax.all_to_all(outgoing, "azi", 0, 0)
    source, down, up = make_source(received, *forward)
    outward = []
    for device in range(count * SECTORS):
        target = device + (1 if device % 2 == 0 else SECTORS - 1)
        if target < count * SECTORS:
            outward.append((device, target))
    axes = ("rad", "azi")
    low = lax.ppermute(up, axes, outward)
    high = lax.ppermute(down, axes, [(target, device) for device, target in outward])
    solved = solve(place, source, low, high, *inverse)
    received = lax.all_to_all(solved.reshape(SECTORS, RANK, LANES), "azi", 0, 0)
    return expand(received, stretch)


def solution(mesh):
    spec = P("rad", "azi", None)
    return jax.shard_map(
        per_device, mesh=mesh, in_specs=(spec,), out_specs=spec, check_vma=False
    )
```

```python
import functools
import math

import jax
import jax.numpy as jnp
import numpy as np
from jax import lax
from jax.experimental import pallas as pl
from jax.experimental.pallas import tpu as pltpu
from jax.sharding import PartitionSpec as P

NPHI = 2048
MODES = 256
SWEEPS = 4
SECTORS = 16
SECTOR = NPHI // SECTORS
COEFS = 2 * MODES
RANK = 48
ROWS = 16
DEPTH = 128
GROUP = 8
LANES = 128
HALF = RANK // 2
BLOCKS = 8
BLOCK_ROWS = 8
EXTENDED = BLOCK_ROWS + 6
CELLS = 3 * GROUP * BLOCK_ROWS
CHUNKS = 4

low_bound = 0.1
high_bound = 2.0
theta = 0.5 * (high_bound + low_bound)
delta = 0.5 * (high_bound - low_bound)
sigma = theta / delta
four_pi = 4.0 * math.pi

BF = jnp.bfloat16
F32 = jnp.float32


def split_table(table):
    high = table.astype(np.float32).astype(BF)
    low = (table - high.astype(np.float64)).astype(np.float32).astype(BF)
    return high, low


@functools.cache
def tables():
    modes = np.arange(MODES)
    angle = 2.0 * np.pi * ((np.arange(SECTOR)[:, None] * modes[None, :]) % NPHI) / NPHI
    first = np.concatenate([np.cos(angle), np.sin(angle)], axis=1)
    left, _, _ = np.linalg.svd(first, full_matrices=False)
    left = left[:, :RANK]
    cores = []
    for sector in range(SECTORS):
        cells = sector * SECTOR + np.arange(SECTOR)
        angle = 2.0 * np.pi * ((cells[:, None] * modes[None, :]) % NPHI) / NPHI
        cores.append(left.T @ np.concatenate([np.cos(angle), np.sin(angle)], axis=1))
    core = np.concatenate(cores, axis=0)
    weight = np.where(np.tile(modes, 2) == 0, 1.0, 2.0)
    left_high, left_low = split_table(left)
    ordered = core.reshape(SECTORS, 2, HALF, COEFS).transpose(1, 0, 2, 3)
    forward = split_table(ordered.reshape(SECTORS * RANK, COEFS) * (-four_pi / NPHI))
    inverse = split_table(core * weight[None, :])
    squeeze = np.concatenate(
        [
            np.concatenate([left_high.T, left_high.T], axis=1),
            np.concatenate([left_low.T, left_low.T], axis=1),
        ],
        axis=0,
    )
    stretch = np.concatenate([left_high, left_high, left_low, left_low], axis=1)
    return squeeze, forward, inverse, stretch


def halves(value):
    high = value.astype(BF)
    low = (value - high.astype(F32)).astype(BF)
    return high, low


def dot(a, b):
    return jnp.dot(a, b, preferred_element_type=F32)


def swap_groups(blocks, size):
    blocks = list(blocks)
    group = lax.broadcasted_iota(jnp.int32, blocks[0].shape, 1) // size
    bit = 1
    while bit < len(blocks):
        keep = (group & bit) == 0
        for i in range(len(blocks)):
            if i & bit:
                continue
            j = i | bit
            one, two = blocks[i], blocks[j]
            blocks[i] = jnp.where(keep, one, pltpu.roll(two, size * bit, 1))
            blocks[j] = jnp.where(keep, pltpu.roll(one, LANES - size * bit, 1), two)
        bit *= 2
    return blocks


def compress_kernel(x_hbm, squeeze_hbm, out_ref, x_ref, squeeze_ref, y_ref, sems):
    table_copy = pltpu.make_async_copy(squeeze_hbm, squeeze_ref, sems.at[CHUNKS])
    table_copy.start()
    rows = ROWS // CHUNKS
    copies = []
    for k in range(CHUNKS):
        part = pl.ds(k * rows, rows)
        copies.append(pltpu.make_async_copy(x_hbm.at[part], x_ref.at[part], sems.at[k]))
        copies[-1].start()
    table_copy.wait()
    squeeze = squeeze_ref[...]
    for r in range(0, ROWS, 2):
        if r % rows == 0:
            copies[r // rows].wait()
        columns = []
        for k in range(2):
            columns.append(jnp.concatenate(halves(x_ref[r + k]), axis=0))
        y = dot(squeeze, jnp.concatenate(columns, axis=1))
        y = y[:RANK] + y[RANK:]
        y_ref[r] = y[:, :LANES]
        y_ref[r + 1] = y[:, LANES:]
    lane = lax.broadcasted_iota(jnp.int32, (8, LANES), 1)
    inside = lane % GROUP
    for c in range(0, HALF, 8):
        pair = []
        for start in (c, c + HALF):
            groups = swap_groups(
                [pltpu.roll(y_ref[r, start : start + 8, :], 4, 1) for r in range(ROWS)], GROUP
            )
            edge = groups[0]
            groups[0] = jnp.where(inside >= 4, edge, 0.0)
            groups.append(jnp.where(inside < 4, edge, 0.0))
            pair.append(groups)
        for g in range(2 * BLOCKS + 1):
            one, two = pair[0][g], pair[1][g]
            packed = (
                jnp.where(lane < 64, one, pltpu.roll(two, 64, 1)),
                jnp.where(lane < 64, pltpu.roll(one, 64, 1), two),
            )
            for j in range(3):
                if (g - j) % 2 or not 0 <= (g - j) // 2 < BLOCKS:
                    continue
                for side in range(2):
                    at = j * HALF + c
                    out_ref[g - j + side, at : at + 8, :] = packed[side]


def source_kernel(place_ref, p_ref, high_ref, low_ref, s_ref, cross_ref, chip_ref):
    turned = []
    for j in range(3):
        block = p_ref[:, j * HALF : (j + 1) * HALF, :].reshape(SECTORS * HALF, LANES).T
        turned.append(jnp.concatenate([block[:64], block[64:]], axis=1))
    cells_high, cells_low = halves(jnp.concatenate(turned, axis=0))
    both = jnp.concatenate([cells_high, cells_low], axis=0)
    for n in range(0, COEFS, 256):
        wide = dot(both, high_ref[:, n : n + 256])
        s_ref[:, n : n + 256] = (
            wide[:CELLS] + wide[CELLS:] + dot(cells_high, low_ref[:, n : n + 256])
        )
    level = lax.broadcasted_iota(jnp.int32, (8, COEFS), 0)

    def at(j, r):
        start = j * 64 + r * 8
        return s_ref[start : start + 8, :]

    def pack(ref, near, middle, far):
        ref[0:8, :] = jnp.where(level < 4, at(2, far), at(0, far))
        ref[8:16, :] = jnp.where(level < 2, pltpu.roll(at(2, middle), 5, 0), at(0, near))
        ref[16:24, :] = at(2, near)
        ref[24:32, :] = jnp.where(level < 3, at(2, middle), at(0, middle))
        ref[32:40, :] = at(1, near)
        ref[40:48, :] = at(1, middle)
        ref[48:56, :] = at(1, far)

    core = place_ref[3]

    @pl.when(core == 0)
    def _():
        pack(cross_ref, 0, 1, 2)
        pack(chip_ref, 7, 6, 5)

    @pl.when(core == 1)
    def _():
        pack(cross_ref, 7, 6, 5)
        pack(chip_ref, 0, 1, 2)


def solve_kernel(
    place_ref,
    s_ref,
    cross_ref,
    chip_ref,
    vh_ref,
    vl_ref,
    out_ref,
    inverse_ref,
    weight_ref,
    own_ref,
    low_ref,
    high_ref,
):
    core = place_ref[3]
    low_ref[...] = jnp.where(core == 0, cross_ref[...], chip_ref[...])
    high_ref[...] = jnp.where(core == 0, chip_ref[...], cross_ref[...])
    shape = (8, LANES)
    level = lax.broadcasted_iota(jnp.int32, shape, 0)
    lane = lax.broadcasted_iota(jnp.int32, shape, 1)
    row_first = place_ref[0]
    row_count = place_ref[1]
    depth_first = place_ref[2]
    bottom = jnp.where(depth_first - 4 + level >= 0, 1.0, 0.0).astype(F32)
    top = jnp.where(depth_first + 12 + level < DEPTH, 1.0, 0.0).astype(F32)

    for e in range(EXTENDED):
        row = jnp.full(shape, row_first + (e - 3), jnp.int32)
        inverse = 1.0 / (row.astype(F32) + 0.5)
        weight_ref[e, 0] = 1.0 + 0.5 * inverse
        weight_ref[e, 1] = 1.0 - 0.5 * inverse
        good = jnp.where((row >= 0) & (row < row_count), 1.0, 0.0).astype(F32)
        for t in range(2):
            ratio = (lane + t * LANES).astype(F32) * inverse
            inverse_ref[t, e] = good / (4.0 + ratio * ratio)

    def turn(value, amount):
        return pltpu.roll(value, amount % 8, 0)

    ratios = []
    ratio = 1.0 / sigma
    for _ in range(SWEEPS - 1):
        following = 1.0 / (2.0 * sigma - ratio)
        ratios.append((following * ratio, 2.0 * following / delta))
        ratio = following

    @pl.loop(0, 4)
    def _(tile):
        lanes = pl.ds(pl.multiple_of(tile * LANES, LANES), LANES)
        table = tile % 2

        def load(ref, start):
            return ref[start : start + 8, lanes]

        def halo(ref, distance):
            if distance == 3:
                both = load(ref, 0)
                return [both, load(ref, 48), both]
            if distance == 2:
                both = load(ref, 24)
                rest = turn(load(ref, 8), 3)
                return [both, load(ref, 40), jnp.where(level < 3, both, rest)]
            return [load(ref, 8), load(ref, 32), load(ref, 16)]

        def source(e):
            if e < 3:
                return halo(low_ref, 3 - e)
            if e >= 11:
                return halo(high_ref, e - 10)
            return [load(s_ref, j * 64 + (e - 3) * 8) for j in range(3)]

        given, scale, step = {}, {}, {}
        state = [{} for _ in range(SWEEPS)]
        for newest in range(EXTENDED + SWEEPS - 1):
            e = newest
            if e < EXTENDED:
                given[e] = source(e)
                middle = inverse_ref[table, e]
                scale[e] = [middle * bottom, middle, middle * top]
                step[e] = [g * i * (1.0 / theta) for g, i in zip(given[e], scale[e])]
                state[0][e] = step[e]
            for sweep in range(1, SWEEPS):
                e = newest - sweep
                if not sweep <= e < EXTENDED - sweep:
                    continue
                keep, push = ratios[sweep - 1]
                old = state[sweep - 1]
                center, outer, inner = old[e], old[e + 1], old[e - 1]
                out_weight, in_weight = weight_ref[e, 0], weight_ref[e, 1]
                above = [turn(x, -1) for x in center]
                below = [turn(x, 1) for x in center]
                steps, values = [], []
                for j in range(3):
                    higher = above[j]
                    if j < 2:
                        higher = jnp.where(level == 7, above[j + 1], higher)
                    lower = below[j]
                    if j > 0:
                        lower = jnp.where(level == 0, below[j - 1], lower)
                    total = given[e][j] + (higher + lower)
                    total = total + (out_weight * outer[j] + in_weight * inner[j])
                    move = keep * step[e][j] + push * (total * scale[e][j] - center[j])
                    steps.append(move)
                    values.append(center[j] + move)
                step[e] = steps
                state[sweep][e] = values
            e = newest - (SWEEPS - 1)
            if 3 <= e < 11:
                x = state[SWEEPS - 1][e]
                at = (e - 3) * 16
                own_ref[at : at + 8, lanes] = turn(jnp.where(level < 4, x[1], x[0]), 4)
                own_ref[at + 8 : at + 16, lanes] = turn(jnp.where(level < 4, x[2], x[1]), 4)

    own_high, own_low = halves(own_ref[...])
    both = jnp.concatenate([own_high, own_low], axis=0)

    def across(a, b):
        return lax.dot_general(a, b, (((1,), (1,)), ((), ())), preferred_element_type=F32)

    step_rows = 192
    for m in range(0, SECTORS * RANK, step_rows):
        wide = across(vh_ref[m : m + step_rows, :], both)
        out_ref[m : m + step_rows, :] = (
            wide[:, :LANES]
            + wide[:, LANES:]
            + across(vl_ref[m : m + step_rows, :], own_high)
        )


def expand_kernel(q_ref, stretch_ref, out_hbm, y_ref, out_ref, sems):
    for side in range(2):
        for c in range(0, RANK, 8):
            rows = swap_groups(
                [q_ref[2 * b + side, c : c + 8, :] for b in range(BLOCKS)], 2 * GROUP
            )
            for r in range(BLOCK_ROWS):
                y_ref[side * BLOCK_ROWS + r, c : c + 8, :] = rows[r]
    stretch = stretch_ref[...]
    rows = ROWS // CHUNKS
    copies = []
    for r in range(0, ROWS, 2):
        columns = []
        for k in range(2):
            high, low = halves(y_ref[r + k])
            columns.append(jnp.concatenate([high, low, high, low], axis=0))
        wide = dot(stretch, jnp.concatenate(columns, axis=1))
        out_ref[r] = wide[:, :LANES]
        out_ref[r + 1] = wide[:, LANES:]
        if (r + 2) % rows == 0:
            part = pl.ds(r + 2 - rows, rows)
            copies.append(
                pltpu.make_async_copy(out_ref.at[part], out_hbm.at[part], sems.at[len(copies)])
            )
            copies[-1].start()
    for copy in copies:
        copy.wait()


VMEM = pl.BlockSpec(memory_space=pltpu.VMEM)
SMEM = pl.BlockSpec(memory_space=pltpu.SMEM)
HBM = pl.BlockSpec(memory_space=pltpu.HBM)


def call(kernel, outs, in_specs, scratch, name, out_space=VMEM, grant=40, **options):
    single = len(outs) == 1
    shapes = [jax.ShapeDtypeStruct(shape, F32) for shape in outs]
    return pl.pallas_call(
        kernel,
        out_shape=shapes[0] if single else shapes,
        in_specs=in_specs,
        out_specs=out_space if single else [out_space] * len(outs),
        scratch_shapes=scratch,
        compiler_params=pltpu.CompilerParams(vmem_limit_bytes=grant * 1024 * 1024),
        name=name,
        **options,
    )


def compress(density, squeeze, **options):
    return call(
        compress_kernel,
        [(SECTORS, 3 * HALF, LANES)],
        [HBM, HBM],
        [
            pltpu.VMEM((ROWS, SECTOR, DEPTH), F32),
            pltpu.VMEM((2 * RANK, 2 * SECTOR), BF),
            pltpu.VMEM((ROWS, RANK, LANES), F32),
            pltpu.SemaphoreType.DMA((CHUNKS + 1,)),
        ],
        "compress",
        grant=62,
        **options,
    )(density, squeeze)


def make_source(place, received, high, low, **options):
    return call(
        source_kernel,
        [(CELLS, COEFS), (56, COEFS), (56, COEFS)],
        [SMEM] + [VMEM] * 3,
        [],
        "make_source",
        **options,
    )(place, received, high, low)


def solve(place, source, cross, chip, v_high, v_low, **options):
    return call(
        solve_kernel,
        [(SECTORS * RANK, LANES)],
        [SMEM] + [VMEM] * 5,
        [
            pltpu.VMEM((2, EXTENDED, 8, LANES), F32),
            pltpu.VMEM((EXTENDED, 2, 8, LANES), F32),
            pltpu.VMEM((LANES, COEFS), F32),
            pltpu.VMEM((56, COEFS), F32),
            pltpu.VMEM((56, COEFS), F32),
        ],
        "solve",
        **options,
    )(place, source, cross, chip, v_high, v_low)


def expand(received, stretch, **options):
    return call(
        expand_kernel,
        [(ROWS, SECTOR, DEPTH)],
        [VMEM] * 2,
        [
            pltpu.VMEM((ROWS, RANK, LANES), F32),
            pltpu.VMEM((ROWS, SECTOR, DEPTH), F32),
            pltpu.SemaphoreType.DMA((CHUNKS,)),
        ],
        "expand",
        out_space=HBM,
        **options,
    )(received, stretch)


def per_device(density):
    squeeze, forward, inverse, stretch = (
        jax.tree.map(jnp.asarray, item) for item in tables()
    )
    count = lax.axis_size("rad")
    azi = lax.axis_index("azi")
    core = azi & 1
    place = jnp.stack(
        [
            lax.axis_index("rad") * ROWS + core * BLOCK_ROWS,
            jnp.int32(count * ROWS),
            (azi >> 1) * 2 * GROUP,
            core,
        ]
    ).astype(jnp.int32)
    outgoing = compress(density, squeeze)
    received = lax.all_to_all(outgoing, "azi", 0, 0)
    source, cross, chip = make_source(place, received, *forward)
    swaps = []
    for device in range(1, (count - 1) * SECTORS, 2):
        swaps += [(device, device + SECTORS - 1), (device + SECTORS - 1, device)]
    cross = lax.ppermute(cross, ("rad", "azi"), swaps)
    chip = lax.ppermute(chip, "azi", [(i, i ^ 1) for i in range(SECTORS)])
    solved = solve(place, source, cross, chip, *inverse)
    received = lax.all_to_all(solved.reshape(SECTORS, RANK, LANES), "azi", 0, 0)
    return expand(received, stretch)


def solution(mesh):
    spec = P("rad", "azi", None)
    return jax.shard_map(
        per_device, mesh=mesh, in_specs=(spec,), out_specs=spec, check_vma=False
    )
```

```python
import functools
import math

import jax
import jax.numpy as jnp
import numpy as np
from jax import lax
from jax.experimental import pallas as pl
from jax.experimental.pallas import tpu as pltpu
from jax.sharding import PartitionSpec as P

NPHI = 2048
MODES = 256
SWEEPS = 4
SECTORS = 16
SECTOR = NPHI // SECTORS
COEFS = 2 * MODES
RANK = 48
ROWS = 16
DEPTH = 128
GROUP = 8
LANES = 128
HALF = RANK // 2
BLOCKS = 8
BLOCK_ROWS = 8
EXTENDED = BLOCK_ROWS + 6
CELLS = 3 * GROUP * BLOCK_ROWS
CHUNKS = 4

low_bound = 0.1
high_bound = 2.0
theta = 0.5 * (high_bound + low_bound)
delta = 0.5 * (high_bound - low_bound)
sigma = theta / delta
four_pi = 4.0 * math.pi

BF = jnp.bfloat16
F32 = jnp.float32


def split_table(table):
    high = table.astype(np.float32).astype(BF)
    low = (table - high.astype(np.float64)).astype(np.float32).astype(BF)
    return high, low


@functools.cache
def tables():
    modes = np.arange(MODES)
    angle = 2.0 * np.pi * ((np.arange(SECTOR)[:, None] * modes[None, :]) % NPHI) / NPHI
    first = np.concatenate([np.cos(angle), np.sin(angle)], axis=1)
    left, _, _ = np.linalg.svd(first, full_matrices=False)
    left = left[:, :RANK]
    cores = []
    for sector in range(SECTORS):
        cells = sector * SECTOR + np.arange(SECTOR)
        angle = 2.0 * np.pi * ((cells[:, None] * modes[None, :]) % NPHI) / NPHI
        cores.append(left.T @ np.concatenate([np.cos(angle), np.sin(angle)], axis=1))
    core = np.concatenate(cores, axis=0)
    weight = np.where(np.tile(modes, 2) == 0, 1.0, 2.0)
    left_high, left_low = split_table(left)
    ordered = core.reshape(SECTORS, 2, HALF, COEFS).transpose(1, 0, 2, 3)
    forward = split_table(ordered.reshape(SECTORS * RANK, COEFS) * (-four_pi / NPHI))
    inverse = split_table(core * weight[None, :])
    squeeze = np.concatenate(
        [
            np.concatenate([left_high.T, left_high.T], axis=1),
            np.concatenate([left_low.T, left_low.T], axis=1),
        ],
        axis=0,
    )
    stretch = np.concatenate([left_high, left_high, left_low, left_low], axis=1)
    return squeeze, forward, inverse, stretch


def halves(value):
    high = value.astype(BF)
    low = (value - high.astype(F32)).astype(BF)
    return high, low


def dot(a, b):
    return jnp.dot(a, b, preferred_element_type=F32)


def swap_groups(blocks, size, bits):
    group = lax.broadcasted_iota(jnp.int32, next(iter(blocks.values())).shape, 1) // size
    for bit in bits:
        keep = (group & bit) == 0
        for i in list(blocks):
            if i & bit:
                continue
            j = i | bit
            one, two = blocks[i], blocks[j]
            blocks[i] = jnp.where(keep, one, pltpu.roll(two, size * bit, 1))
            blocks[j] = jnp.where(keep, pltpu.roll(one, LANES - size * bit, 1), two)
    return blocks


def compress_kernel(high_ref, low_ref, squeeze_ref, out_ref, y_ref):
    squeeze = squeeze_ref[...]
    for r in range(0, ROWS, 2):
        rows = slice(r, r + 2)
        pair = [jnp.concatenate([h, l], axis=0) for h, l in zip(high_ref[rows], low_ref[rows])]
        y = dot(squeeze, jnp.concatenate(pair, axis=1))
        y = y[:RANK] + y[RANK:]
        y_ref[r] = y[:, :LANES]
        y_ref[r + 1] = y[:, LANES:]
    for side in range(2):
        first = side * BLOCK_ROWS
        for c in range(0, HALF, 8):
            blocks = {}
            for r in range(BLOCK_ROWS):
                for half in range(2):
                    start = half * HALF + c
                    blocks[half * BLOCK_ROWS + r] = y_ref[first + r, start : start + 8, :]
            swap_groups(blocks, GROUP, (1, 2, 4, 8))
            for g in blocks:
                for j in range(g % 2, 3, 2):
                    at = j * HALF + c
                    out_ref[(g - j) % SECTORS + side, at : at + 8, :] = blocks[g]


def source_kernel(p_ref, high_ref, low_ref, s_ref, cross_ref, chip_ref):
    turned = []
    for j in range(3):
        block = p_ref[:, j * HALF : (j + 1) * HALF, :].reshape(SECTORS * HALF, LANES).T
        turned.append(jnp.concatenate([block[:64], block[64:]], axis=1))
    cells_high, cells_low = halves(jnp.concatenate(turned, axis=0))
    both = jnp.concatenate([cells_high, cells_low], axis=0)
    for n in range(0, COEFS, 256):
        wide = dot(both, high_ref[:, n : n + 256])
        s_ref[:, n : n + 256] = (
            wide[:CELLS] + wide[CELLS:] + dot(cells_high, low_ref[:, n : n + 256])
        )
    level = lax.broadcasted_iota(jnp.int32, (8, COEFS), 0)

    def at(j, r):
        return s_ref[pl.ds(pl.multiple_of(j * 64 + r * 8, 8), 8), :]

    def pack(ref, near, middle, far):
        ref[0:8, :] = jnp.where(level < 4, at(2, far), at(0, far))
        ref[8:16, :] = jnp.where(level < 2, pltpu.roll(at(2, middle), 5, 0), at(0, near))
        ref[16:24, :] = at(2, near)
        ref[24:32, :] = jnp.where(level < 3, at(2, middle), at(0, middle))
        ref[32:40, :] = at(1, near)
        ref[40:48, :] = at(1, middle)
        ref[48:56, :] = at(1, far)

    core = lax.axis_index("azi") & 1
    start, back = core * 7, 1 - 2 * core
    pack(cross_ref, start, start + back, start + 2 * back)
    start, back = 7 - start, -back
    pack(chip_ref, start, start + back, start + 2 * back)


def unpack(load, distance, level):
    if distance == 3:
        both = load(0)
        return [both, load(48), both]
    if distance == 2:
        both = load(24)
        rest = pltpu.roll(load(8), 3, 0)
        return [both, load(40), jnp.where(level < 3, both, rest)]
    return [load(8), load(32), load(16)]


def factors():
    steps = []
    ratio = 1.0 / sigma
    for _ in range(SWEEPS - 1):
        following = 1.0 / (2.0 * sigma - ratio)
        steps.append((following * ratio, 2.0 * following / delta))
        ratio = following
    return steps


def vertical(center, level, cut):
    above = [pltpu.roll(x, 7, 0) for x in center]
    below = [pltpu.roll(x, 1, 0) for x in center]
    return [
        jnp.where(level == 7, above[1], above[0]) + below[0],
        jnp.where(level == 7, above[2] * cut, above[1])
        + jnp.where(level == 0, below[0], below[1]),
        above[2] + jnp.where(level == 0, below[1] * cut, below[2]),
    ]


def window_cut():
    last = (lax.axis_index("azi") >> 1) == BLOCKS - 1
    return jnp.where(jnp.full((8, LANES), last), 0.0, 1.0).astype(F32)


def main_kernel(count, s_ref, own_ref, inverse_ref, weight_ref):
    shape = (8, LANES)
    level = lax.broadcasted_iota(jnp.int32, shape, 0)
    lane = lax.broadcasted_iota(jnp.int32, shape, 1)
    core = lax.axis_index("azi") & 1
    row_first = lax.axis_index("rad") * ROWS + core * BLOCK_ROWS
    cut = window_cut()

    for e in range(EXTENDED):
        row = jnp.full(shape, row_first + (e - 3), jnp.int32)
        inverse = 1.0 / (row.astype(F32) + 0.5)
        weight_ref[e, 0] = 1.0 + 0.5 * inverse
        weight_ref[e, 1] = 1.0 - 0.5 * inverse
        good = jnp.where((row >= 0) & (row < count * ROWS), 1.0, 0.0).astype(F32)
        for t in range(2):
            ratio = (lane + t * LANES).astype(F32) * inverse
            inverse_ref[t, e] = good / (4.0 + ratio * ratio)

    ratios = factors()

    @pl.loop(0, 4)
    def _(tile):
        lanes = pl.ds(pl.multiple_of(tile * LANES, LANES), LANES)
        table = tile % 2
        given, scale, step = {}, {}, {}
        state = [{} for _ in range(SWEEPS)]
        for newest in range(3, EXTENDED + SWEEPS - 1):
            e = newest
            if e < 11:
                starts = [j * 64 + (e - 3) * 8 for j in range(3)]
                given[e] = [s_ref[start : start + 8, lanes] for start in starts]
                scale[e] = inverse_ref[table, e]
                step[e] = [g * scale[e] * (1.0 / theta) for g in given[e]]
                state[0][e] = step[e]
            for sweep in range(1, SWEEPS):
                e = newest - sweep
                reach = min(sweep, SWEEPS - 1 - sweep)
                if not 3 - reach <= e < 11 + reach:
                    continue
                keep, push = ratios[sweep - 1]
                steps, values = advance(
                    keep,
                    push,
                    state[sweep - 1],
                    given.get(e),
                    step.get(e),
                    e,
                    inverse_ref[table, e],
                    weight_ref[e, 0],
                    weight_ref[e, 1],
                    level,
                    cut,
                )
                step[e] = steps
                state[sweep][e] = values
            e = newest - (SWEEPS - 1)
            if 3 <= e < 11:
                x = state[SWEEPS - 1][e]
                at = (e - 3) * 16
                own_ref[at : at + 8, lanes] = jnp.where(level < 4, x[2], x[0])
                own_ref[at + 8 : at + 16, lanes] = x[1]


def advance(keep, push, old, given, step, e, scale, plus, minus, level, cut):
    center = old.get(e)
    near = vertical(center, level, cut) if center is not None else None
    steps, values = [], []
    for j in range(3):
        terms = []
        if given is not None:
            terms.append(given[j])
        if near is not None:
            terms.append(near[j])
        if e + 1 in old:
            terms.append(plus * old[e + 1][j])
        if e - 1 in old:
            terms.append(minus * old[e - 1][j])
        move = (push * scale) * sum(terms[1:], terms[0])
        if center is not None:
            move = move - push * center[j]
        if step is not None:
            move = move + keep * step[j]
        steps.append(move)
        values.append(move if center is None else center[j] + move)
    return steps, values


def edge_kernel(
    main_ref, inverse_ref, weight_ref, cross_ref, chip_ref, vh_ref, vl_ref, out_ref, own_ref
):
    level = lax.broadcasted_iota(jnp.int32, (8, LANES), 0)
    core = lax.axis_index("azi") & 1
    cut = window_cut()
    ratios = factors()
    own_ref[...] = main_ref[...]

    @pl.loop(0, 4)
    def _(tile):
        lanes = pl.ds(pl.multiple_of(tile * LANES, LANES), LANES)
        table = tile % 2
        for ref, turned in ((cross_ref, core), (chip_ref, 1 - core)):
            at = [t + turned * (EXTENDED - 1 - 2 * t) for t in range(6)]
            given = {
                t: unpack(lambda start: ref[start : start + 8, lanes], 3 - t, level)
                for t in range(3)
            }
            scale = [inverse_ref[table, e] for e in at]
            step = {t: [g * scale[t] * (1.0 / theta) for g in given[t]] for t in given}
            state = dict(step)
            for sweep in range(1, SWEEPS):
                keep, push = ratios[sweep - 1]
                fresh = {}
                for t in range(sweep, sweep + 3):
                    steps, fresh[t] = advance(
                        keep,
                        push,
                        state,
                        given.get(t),
                        step.get(t),
                        t,
                        scale[t],
                        weight_ref[at[t], turned],
                        weight_ref[at[t], 1 - turned],
                        level,
                        cut,
                    )
                    step[t] = steps
                state = fresh
            for t in range(3, 6):
                x = state[t]
                start = pl.multiple_of((at[t] - 3) * 16, 16)
                own_ref[pl.ds(start, 8), lanes] += jnp.where(level < 4, x[2], x[0])
                own_ref[pl.ds(start + 8, 8), lanes] += x[1]

    own_high, own_low = halves(own_ref[...])
    both = jnp.concatenate([own_high, own_low], axis=0)

    def across(a, b):
        return lax.dot_general(a, b, (((1,), (1,)), ((), ())), preferred_element_type=F32)

    step_rows = 192
    for m in range(0, SECTORS * RANK, step_rows):
        wide = across(vh_ref[m : m + step_rows, :], both)
        out_ref[m : m + step_rows, :] = (
            wide[:, :LANES]
            + wide[:, LANES:]
            + across(vl_ref[m : m + step_rows, :], own_high)
        )


def expand_kernel(q_ref, stretch_ref, out_hbm, y_ref, out_ref, sems):
    stretch = stretch_ref[...]
    first = lax.broadcasted_iota(jnp.int32, (8, LANES), 1) % (2 * GROUP) < 4
    rows = ROWS // CHUNKS
    copies = []
    for side in range(2):
        for c in range(0, RANK, 8):
            held = [q_ref[2 * b + side, c : c + 8, :] for b in range(BLOCKS)]
            blocks = {b: jnp.where(first, held[b - 1], held[b]) for b in range(BLOCKS)}
            swap_groups(blocks, 2 * GROUP, (1, 2, 4))
            for r in range(BLOCK_ROWS):
                y_ref[side * BLOCK_ROWS + r, c : c + 8, :] = blocks[r]
        for r in range(side * BLOCK_ROWS, (side + 1) * BLOCK_ROWS, 2):
            columns = []
            for k in range(2):
                high, low = halves(y_ref[r + k])
                columns.append(jnp.concatenate([high, low, high, low], axis=0))
            wide = dot(stretch, jnp.concatenate(columns, axis=1))
            out_ref[r] = wide[:, :LANES]
            out_ref[r + 1] = wide[:, LANES:]
            if (r + 2) % rows == 0:
                part = pl.ds(r + 2 - rows, rows)
                sem = sems.at[len(copies)]
                copies.append(pltpu.make_async_copy(out_ref.at[part], out_hbm.at[part], sem))
                copies[-1].start()
    for copy in copies:
        copy.wait()


VMEM = pl.BlockSpec(memory_space=pltpu.VMEM)
HBM = pl.BlockSpec(memory_space=pltpu.HBM)


def call(kernel, outs, in_specs, scratch, name, out_space=VMEM, **options):
    single = len(outs) == 1
    shapes = [jax.ShapeDtypeStruct(shape, F32) for shape in outs]
    return pl.pallas_call(
        kernel,
        out_shape=shapes[0] if single else shapes,
        in_specs=in_specs,
        out_specs=out_space if single else [out_space] * len(outs),
        scratch_shapes=scratch,
        compiler_params=pltpu.CompilerParams(vmem_limit_bytes=40 * 1024 * 1024),
        name=name,
        **options,
    )


def compress(high, low, squeeze, **options):
    return call(
        compress_kernel,
        [(SECTORS, 3 * HALF, LANES)],
        [VMEM] * 3,
        [pltpu.VMEM((ROWS, RANK, LANES), F32)],
        "compress",
        **options,
    )(high, low, squeeze)


def make_source(received, high, low, **options):
    return call(
        source_kernel,
        [(CELLS, COEFS), (56, COEFS), (56, COEFS)],
        [VMEM] * 3,
        [],
        "make_source",
        **options,
    )(received, high, low)


def solve_main(count, source, **options):
    return call(
        functools.partial(main_kernel, count),
        [(LANES, COEFS), (2, EXTENDED, 8, LANES), (EXTENDED, 2, 8, LANES)],
        [VMEM],
        [],
        "solve_main",
        cost_estimate=pl.CostEstimate(
            flops=40_000_000, bytes_accessed=1_000_000, transcendentals=0
        ),
        **options,
    )(source)


def solve_edge(main, inverse, weight, cross, chip, v_high, v_low, **options):
    return call(
        edge_kernel,
        [(SECTORS * RANK, LANES)],
        [VMEM] * 7,
        [pltpu.VMEM((LANES, COEFS), F32)],
        "solve_edge",
        **options,
    )(main, inverse, weight, cross, chip, v_high, v_low)


def expand(received, stretch, **options):
    return call(
        expand_kernel,
        [(ROWS, SECTOR, DEPTH)],
        [VMEM] * 2,
        [
            pltpu.VMEM((ROWS, RANK, LANES), F32),
            pltpu.VMEM((ROWS, SECTOR, DEPTH), F32),
            pltpu.SemaphoreType.DMA((CHUNKS,)),
        ],
        "expand",
        out_space=HBM,
        **options,
    )(received, stretch)


def split_rows(density):
    high = lax.reduce_precision(density, 8, 7)
    return high.astype(BF), (density - high).astype(BF)


def per_device(density):
    squeeze, forward, inverse, stretch = (
        jax.tree.map(jnp.asarray, item) for item in tables()
    )
    count = lax.axis_size("rad")
    outgoing = compress(*split_rows(density), squeeze)
    received = lax.all_to_all(outgoing, "azi", 0, 0)
    source, cross, chip = make_source(received, *forward)
    swaps = []
    for device in range(1, (count - 1) * SECTORS, 2):
        swaps += [(device, device + SECTORS - 1), (device + SECTORS - 1, device)]
    cross = lax.ppermute(cross, ("rad", "azi"), swaps)
    chip = lax.ppermute(chip, "azi", [(i, i ^ 1) for i in range(SECTORS)])
    main, scales, weights = solve_main(count, source)
    solved = solve_edge(main, scales, weights, cross, chip, *inverse)
    received = lax.all_to_all(solved.reshape(SECTORS, RANK, LANES), "azi", 0, 0)
    return expand(received, stretch)


def solution(mesh):
    spec = P("rad", "azi", None)
    return jax.shard_map(
        per_device, mesh=mesh, in_specs=(spec,), out_specs=spec, check_vma=False
    )
```

```python
import functools
import math

import jax
import jax.numpy as jnp
import numpy as np
from jax import lax
from jax.experimental import pallas as pl
from jax.experimental.pallas import tpu as pltpu
from jax.sharding import PartitionSpec as P

NPHI = 2048
MODES = 256
SWEEPS = 4
SECTORS = 16
SECTOR = NPHI // SECTORS
COEFS = 2 * MODES
RANK = 48
ROWS = 16
DEPTH = 128
GROUP = 8
LANES = 128
HALF = RANK // 2
BLOCKS = 8
BLOCK_ROWS = 8
EXTENDED = BLOCK_ROWS + 6
CELLS = 3 * GROUP * BLOCK_ROWS
CHUNKS = 4

low_bound = 0.1
high_bound = 2.0
theta = 0.5 * (high_bound + low_bound)
delta = 0.5 * (high_bound - low_bound)
sigma = theta / delta
four_pi = 4.0 * math.pi

BF = jnp.bfloat16
F32 = jnp.float32


def split_table(table):
    high = table.astype(np.float32).astype(BF)
    low = (table - high.astype(np.float64)).astype(np.float32).astype(BF)
    return high, low


@functools.cache
def tables():
    modes = np.arange(MODES)
    angle = 2.0 * np.pi * ((np.arange(SECTOR)[:, None] * modes[None, :]) % NPHI) / NPHI
    first = np.concatenate([np.cos(angle), np.sin(angle)], axis=1)
    left, _, _ = np.linalg.svd(first, full_matrices=False)
    left = left[:, :RANK]
    cores = []
    for sector in range(SECTORS):
        cells = sector * SECTOR + np.arange(SECTOR)
        angle = 2.0 * np.pi * ((cells[:, None] * modes[None, :]) % NPHI) / NPHI
        cores.append(left.T @ np.concatenate([np.cos(angle), np.sin(angle)], axis=1))
    core = np.concatenate(cores, axis=0)
    weight = np.where(np.tile(modes, 2) == 0, 1.0, 2.0)
    left_high, left_low = split_table(left)
    ordered = core.reshape(SECTORS, 2, HALF, COEFS).transpose(1, 0, 2, 3)
    forward = split_table(ordered.reshape(SECTORS * RANK, COEFS) * (-four_pi / NPHI))
    inverse = split_table(core * weight[None, :])
    squeeze = np.concatenate(
        [
            np.concatenate([left_high.T, left_high.T], axis=1),
            np.concatenate([left_low.T, left_low.T], axis=1),
        ],
        axis=0,
    )
    stretch = np.concatenate([left_high, left_high, left_low, left_low], axis=1)
    return squeeze, forward, inverse, stretch


def halves(value):
    high = value.astype(BF)
    low = (value - high.astype(F32)).astype(BF)
    return high, low


def dot(a, b):
    return jnp.dot(a, b, preferred_element_type=F32)


def swap_groups(blocks, size, bits):
    group = lax.broadcasted_iota(jnp.int32, next(iter(blocks.values())).shape, 1) // size
    for bit in bits:
        keep = (group & bit) == 0
        for i in list(blocks):
            if i & bit:
                continue
            j = i | bit
            one, two = blocks[i], blocks[j]
            if 2 * size * bit == LANES:
                up = down = pltpu.roll(jnp.where(keep, two, one), LANES // 2, 1)
            else:
                up = pltpu.roll(two, size * bit, 1)
                down = pltpu.roll(one, LANES - size * bit, 1)
            blocks[i] = jnp.where(keep, one, up)
            blocks[j] = jnp.where(keep, down, two)
    return blocks


def compress_kernel(high_ref, low_ref, squeeze_ref, out_ref, y_ref):
    squeeze = squeeze_ref[...]
    for r in range(0, ROWS, 2):
        rows = slice(r, r + 2)
        pair = [jnp.concatenate([h, l], axis=0) for h, l in zip(high_ref[rows], low_ref[rows])]
        y = dot(squeeze, jnp.concatenate(pair, axis=1))
        y = y[:RANK] + y[RANK:]
        y_ref[r] = y[:, :LANES]
        y_ref[r + 1] = y[:, LANES:]
    for side in range(2):
        first = side * BLOCK_ROWS
        for c in range(0, HALF, 8):
            blocks = {}
            for r in range(BLOCK_ROWS):
                for half in range(2):
                    start = half * HALF + c
                    blocks[half * BLOCK_ROWS + r] = y_ref[first + r, start : start + 8, :]
            swap_groups(blocks, GROUP, (1, 2, 4, 8))
            for g in blocks:
                for j in range(g % 2, 3, 2):
                    at = j * HALF + c
                    out_ref[(g - j) % SECTORS + side, at : at + 8, :] = blocks[g]


def source_kernel(p_ref, high_ref, low_ref, s_ref, cross_ref, chip_ref):
    turned = []
    for j in range(3):
        block = p_ref[:, j * HALF : (j + 1) * HALF, :].reshape(SECTORS * HALF, LANES).T
        turned.append(jnp.concatenate([block[:64], block[64:]], axis=1))
    cells_high, cells_low = halves(jnp.concatenate(turned, axis=0))
    both = jnp.concatenate([cells_high, cells_low], axis=0)
    for n in range(0, COEFS, 256):
        wide = dot(both, high_ref[:, n : n + 256])
        s_ref[:, n : n + 256] = (
            wide[:CELLS] + wide[CELLS:] + dot(cells_high, low_ref[:, n : n + 256])
        )
    level = lax.broadcasted_iota(jnp.int32, (8, COEFS), 0)

    def at(j, r):
        return s_ref[pl.ds(pl.multiple_of(j * 64 + r * 8, 8), 8), :]

    def pack(ref, near, middle, far):
        ref[0:8, :] = jnp.where(level < 4, at(2, far), at(0, far))
        ref[8:16, :] = jnp.where(level < 2, pltpu.roll(at(2, middle), 5, 0), at(0, near))
        ref[16:24, :] = at(2, near)
        ref[24:32, :] = jnp.where(level < 3, at(2, middle), at(0, middle))
        ref[32:40, :] = at(1, near)
        ref[40:48, :] = at(1, middle)
        ref[48:56, :] = at(1, far)

    core = lax.axis_index("azi") & 1
    start, back = core * 7, 1 - 2 * core
    pack(cross_ref, start, start + back, start + 2 * back)
    start, back = 7 - start, -back
    pack(chip_ref, start, start + back, start + 2 * back)


def unpack(load, distance, level):
    if distance == 3:
        both = load(0)
        return [both, load(48), both]
    if distance == 2:
        both = load(24)
        rest = pltpu.roll(load(8), 3, 0)
        return [both, load(40), jnp.where(level < 3, both, rest)]
    return [load(8), load(32), load(16)]


def factors():
    steps = []
    ratio = 1.0 / sigma
    for _ in range(SWEEPS - 1):
        following = 1.0 / (2.0 * sigma - ratio)
        steps.append((following * ratio, 2.0 * following / delta))
        ratio = following
    return steps


def vertical(center, level, cut):
    above = [pltpu.roll(x, 7, 0) for x in center]
    below = [pltpu.roll(x, 1, 0) for x in center]
    return [
        jnp.where(level == 7, above[1], above[0]) + below[0],
        jnp.where(level == 7, above[2] * cut, above[1])
        + jnp.where(level == 0, below[0], below[1]),
        above[2] + jnp.where(level == 0, below[1] * cut, below[2]),
    ]


def window_cut():
    last = (lax.axis_index("azi") >> 1) == BLOCKS - 1
    return jnp.where(jnp.full((8, LANES), last), 0.0, 1.0).astype(F32)


def main_kernel(count, s_ref, own_ref, inverse_ref, weight_ref):
    shape = (8, LANES)
    level = lax.broadcasted_iota(jnp.int32, shape, 0)
    lane = lax.broadcasted_iota(jnp.int32, shape, 1)
    core = lax.axis_index("azi") & 1
    row_first = lax.axis_index("rad") * ROWS + core * BLOCK_ROWS
    cut = window_cut()

    for e in range(EXTENDED):
        row = jnp.full(shape, row_first + (e - 3), jnp.int32)
        inverse = 1.0 / (row.astype(F32) + 0.5)
        weight_ref[e, 0] = 1.0 + 0.5 * inverse
        weight_ref[e, 1] = 1.0 - 0.5 * inverse
        good = jnp.where((row >= 0) & (row < count * ROWS), 1.0, 0.0).astype(F32)
        for t in range(2):
            ratio = (lane + t * LANES).astype(F32) * inverse
            inverse_ref[t, e] = good / (4.0 + ratio * ratio)

    ratios = factors()

    @pl.loop(0, 4)
    def _(tile):
        lanes = pl.ds(pl.multiple_of(tile * LANES, LANES), LANES)
        table = tile % 2
        given, scale, step = {}, {}, {}
        state = [{} for _ in range(SWEEPS)]
        for newest in range(3, EXTENDED + SWEEPS - 1):
            e = newest
            if e < 11:
                starts = [j * 64 + (e - 3) * 8 for j in range(3)]
                given[e] = [s_ref[start : start + 8, lanes] for start in starts]
                scale[e] = inverse_ref[table, e]
                step[e] = [g * scale[e] * (1.0 / theta) for g in given[e]]
                state[0][e] = step[e]
            for sweep in range(1, SWEEPS):
                e = newest - sweep
                reach = min(sweep, SWEEPS - 1 - sweep)
                if not 3 - reach <= e < 11 + reach:
                    continue
                keep, push = ratios[sweep - 1]
                steps, values = advance(
                    keep,
                    push,
                    state[sweep - 1],
                    given.get(e),
                    step.get(e),
                    e,
                    inverse_ref[table, e],
                    weight_ref[e, 0],
                    weight_ref[e, 1],
                    level,
                    cut,
                )
                step[e] = steps
                state[sweep][e] = values
            e = newest - (SWEEPS - 1)
            if 3 <= e < 11:
                x = state[SWEEPS - 1][e]
                at = (e - 3) * 16
                own_ref[at : at + 8, lanes] = jnp.where(level < 4, x[2], x[0])
                own_ref[at + 8 : at + 16, lanes] = x[1]


def advance(keep, push, old, given, step, e, scale, plus, minus, level, cut):
    center = old.get(e)
    near = vertical(center, level, cut) if center is not None else None
    steps, values = [], []
    for j in range(3):
        terms = []
        if given is not None:
            terms.append(given[j])
        if near is not None:
            terms.append(near[j])
        if e + 1 in old:
            terms.append(plus * old[e + 1][j])
        if e - 1 in old:
            terms.append(minus * old[e - 1][j])
        move = (push * scale) * sum(terms[1:], terms[0])
        if center is not None:
            move = move - push * center[j]
        if step is not None:
            move = move + keep * step[j]
        steps.append(move)
        values.append(move if center is None else center[j] + move)
    return steps, values


def edge_kernel(
    main_ref, inverse_ref, weight_ref, cross_ref, chip_ref, vh_ref, vl_ref, out_ref, own_ref
):
    level = lax.broadcasted_iota(jnp.int32, (8, LANES), 0)
    core = lax.axis_index("azi") & 1
    cut = window_cut()
    ratios = factors()
    own_ref[...] = main_ref[...]

    @pl.loop(0, 4, unroll=4)
    def _(tile):
        lanes = pl.ds(pl.multiple_of(tile * LANES, LANES), LANES)
        table = tile % 2
        for ref, turned in ((cross_ref, core), (chip_ref, 1 - core)):
            at = [t + turned * (EXTENDED - 1 - 2 * t) for t in range(6)]
            given = {
                t: unpack(lambda start: ref[start : start + 8, lanes], 3 - t, level)
                for t in range(3)
            }
            scale = [inverse_ref[table, e] for e in at]
            step = {t: [g * scale[t] * (1.0 / theta) for g in given[t]] for t in given}
            state = dict(step)
            for sweep in range(1, SWEEPS):
                keep, push = ratios[sweep - 1]
                fresh = {}
                for t in range(sweep, sweep + 3):
                    steps, fresh[t] = advance(
                        keep,
                        push,
                        state,
                        given.get(t),
                        step.get(t),
                        t,
                        scale[t],
                        weight_ref[at[t], turned],
                        weight_ref[at[t], 1 - turned],
                        level,
                        cut,
                    )
                    step[t] = steps
                state = fresh
            for t in range(3, 6):
                x = state[t]
                start = pl.multiple_of((at[t] - 3) * 16, 16)
                own_ref[pl.ds(start, 8), lanes] += jnp.where(level < 4, x[2], x[0])
                own_ref[pl.ds(start + 8, 8), lanes] += x[1]

    own_high, own_low = halves(own_ref[...])
    both = jnp.concatenate([own_high, own_low], axis=0)

    def across(a, b):
        return lax.dot_general(a, b, (((1,), (1,)), ((), ())), preferred_element_type=F32)

    step_rows = 384
    for m in range(0, SECTORS * RANK, step_rows):
        wide = across(vh_ref[m : m + step_rows, :], both)
        out_ref[m : m + step_rows, :] = (
            wide[:, :LANES]
            + wide[:, LANES:]
            + across(vl_ref[m : m + step_rows, :], own_high)
        )


def expand_kernel(q_ref, stretch_ref, out_hbm, y_ref, out_ref, sems):
    stretch = stretch_ref[...]
    first = lax.broadcasted_iota(jnp.int32, (8, LANES), 1) % (2 * GROUP) < 4
    rows = ROWS // CHUNKS
    copies = []
    for side in range(2):
        for c in range(0, RANK, 8):
            held = [q_ref[2 * b + side, c : c + 8, :] for b in range(BLOCKS)]
            blocks = {b: jnp.where(first, held[b - 1], held[b]) for b in range(BLOCKS)}
            swap_groups(blocks, 2 * GROUP, (1, 2, 4))
            for r in range(BLOCK_ROWS):
                y_ref[side * BLOCK_ROWS + r, c : c + 8, :] = blocks[r]
        for r in range(side * BLOCK_ROWS, (side + 1) * BLOCK_ROWS, 2):
            columns = []
            for k in range(2):
                high, low = halves(y_ref[r + k])
                columns.append(jnp.concatenate([high, low, high, low], axis=0))
            wide = dot(stretch, jnp.concatenate(columns, axis=1))
            out_ref[r] = wide[:, :LANES]
            out_ref[r + 1] = wide[:, LANES:]
            if (r + 2) % rows == 0:
                part = pl.ds(r + 2 - rows, rows)
                sem = sems.at[len(copies)]
                copies.append(pltpu.make_async_copy(out_ref.at[part], out_hbm.at[part], sem))
                copies[-1].start()
    for copy in copies:
        copy.wait()


VMEM = pl.BlockSpec(memory_space=pltpu.VMEM)
HBM = pl.BlockSpec(memory_space=pltpu.HBM)


def call(kernel, outs, in_specs, scratch, name, out_space=VMEM, **options):
    single = len(outs) == 1
    shapes = [jax.ShapeDtypeStruct(shape, F32) for shape in outs]
    return pl.pallas_call(
        kernel,
        out_shape=shapes[0] if single else shapes,
        in_specs=in_specs,
        out_specs=out_space if single else [out_space] * len(outs),
        scratch_shapes=scratch,
        compiler_params=pltpu.CompilerParams(vmem_limit_bytes=40 * 1024 * 1024),
        name=name,
        **options,
    )


def compress(high, low, squeeze, **options):
    return call(
        compress_kernel,
        [(SECTORS, 3 * HALF, LANES)],
        [VMEM] * 3,
        [pltpu.VMEM((ROWS, RANK, LANES), F32)],
        "compress",
        **options,
    )(high, low, squeeze)


def make_source(received, high, low, **options):
    return call(
        source_kernel,
        [(CELLS, COEFS), (56, COEFS), (56, COEFS)],
        [VMEM] * 3,
        [],
        "make_source",
        **options,
    )(received, high, low)


def solve_main(count, source, **options):
    return call(
        functools.partial(main_kernel, count),
        [(LANES, COEFS), (2, EXTENDED, 8, LANES), (EXTENDED, 2, 8, LANES)],
        [VMEM],
        [],
        "solve_main",
        cost_estimate=pl.CostEstimate(
            flops=40_000_000, bytes_accessed=1_000_000, transcendentals=0
        ),
        **options,
    )(source)


def solve_edge(main, inverse, weight, cross, chip, v_high, v_low, **options):
    return call(
        edge_kernel,
        [(SECTORS * RANK, LANES)],
        [VMEM] * 7,
        [pltpu.VMEM((LANES, COEFS), F32)],
        "solve_edge",
        **options,
    )(main, inverse, weight, cross, chip, v_high, v_low)


def expand(received, stretch, **options):
    return call(
        expand_kernel,
        [(ROWS, SECTOR, DEPTH)],
        [VMEM] * 2,
        [
            pltpu.VMEM((ROWS, RANK, LANES), F32),
            pltpu.VMEM((ROWS, SECTOR, DEPTH), F32),
            pltpu.SemaphoreType.DMA((CHUNKS,)),
        ],
        "expand",
        out_space=HBM,
        **options,
    )(received, stretch)


def split_rows(density):
    high = lax.reduce_precision(density, 8, 7)
    return high.astype(BF), (density - high).astype(BF)


def per_device(density):
    squeeze, forward, inverse, stretch = (
        jax.tree.map(jnp.asarray, item) for item in tables()
    )
    count = lax.axis_size("rad")
    outgoing = compress(*split_rows(density), squeeze)
    received = lax.all_to_all(outgoing, "azi", 0, 0)
    source, cross, chip = make_source(received, *forward)
    swaps = []
    for device in range(1, (count - 1) * SECTORS, 2):
        swaps += [(device, device + SECTORS - 1), (device + SECTORS - 1, device)]
    cross = lax.ppermute(cross, ("rad", "azi"), swaps)
    chip = lax.ppermute(chip, "azi", [(i, i ^ 1) for i in range(SECTORS)])
    main, scales, weights = solve_main(count, source)
    solved = solve_edge(main, scales, weights, cross, chip, *inverse)
    received = lax.all_to_all(solved.reshape(SECTORS, RANK, LANES), "azi", 0, 0)
    return expand(received, stretch)


def solution(mesh):
    spec = P("rad", "azi", None)
    return jax.shard_map(
        per_device, mesh=mesh, in_specs=(spec,), out_specs=spec, check_vma=False
    )
```

```python
import functools
import math

import jax
import jax.numpy as jnp
import numpy as np
from jax import lax
from jax.experimental import pallas as pl
from jax.experimental.pallas import tpu as pltpu
from jax.sharding import PartitionSpec as P

NPHI = 2048
MODES = 256
SWEEPS = 4
SECTORS = 16
SECTOR = NPHI // SECTORS
COEFS = 2 * MODES
RANK = 48
ROWS = 16
DEPTH = 128
GROUP = 8
LANES = 128
HALF = RANK // 2
BLOCKS = 8
BLOCK_ROWS = 8
EXTENDED = BLOCK_ROWS + 6
CELLS = 3 * GROUP * BLOCK_ROWS
CHUNKS = 4

low_bound = 0.1
high_bound = 2.0
theta = 0.5 * (high_bound + low_bound)
delta = 0.5 * (high_bound - low_bound)
sigma = theta / delta
four_pi = 4.0 * math.pi

BF = jnp.bfloat16
F32 = jnp.float32


def split_table(table):
    high = table.astype(np.float32).astype(BF)
    low = (table - high.astype(np.float64)).astype(np.float32).astype(BF)
    return high, low


@functools.cache
def tables():
    modes = np.arange(MODES)
    angle = 2.0 * np.pi * ((np.arange(SECTOR)[:, None] * modes[None, :]) % NPHI) / NPHI
    first = np.concatenate([np.cos(angle), np.sin(angle)], axis=1)
    left, _, _ = np.linalg.svd(first, full_matrices=False)
    left = left[:, :RANK]
    cores = []
    for sector in range(SECTORS):
        cells = sector * SECTOR + np.arange(SECTOR)
        angle = 2.0 * np.pi * ((cells[:, None] * modes[None, :]) % NPHI) / NPHI
        cores.append(left.T @ np.concatenate([np.cos(angle), np.sin(angle)], axis=1))
    core = np.concatenate(cores, axis=0)
    weight = np.where(np.tile(modes, 2) == 0, 1.0, 2.0)
    left_high, left_low = split_table(left)
    ordered = core.reshape(SECTORS, 2, HALF, COEFS).transpose(1, 0, 2, 3)
    forward = split_table(ordered.reshape(SECTORS * RANK, COEFS) * (-four_pi / NPHI))
    inverse = split_table(core * weight[None, :])
    squeeze = np.concatenate(
        [
            np.concatenate([left_high.T, left_high.T], axis=1),
            np.concatenate([left_low.T, left_low.T], axis=1),
        ],
        axis=0,
    )
    stretch = np.concatenate([left_high, left_high, left_low, left_low], axis=1)
    return squeeze, forward, inverse, stretch


def halves(value):
    high = value.astype(BF)
    low = (value - high.astype(F32)).astype(BF)
    return high, low


def dot(a, b):
    return jnp.dot(a, b, preferred_element_type=F32)


def swap_groups(blocks, size, bits):
    group = lax.broadcasted_iota(jnp.int32, next(iter(blocks.values())).shape, 1) // size
    for bit in bits:
        keep = (group & bit) == 0
        for i in list(blocks):
            if i & bit:
                continue
            j = i | bit
            one, two = blocks[i], blocks[j]
            if 2 * size * bit == LANES:
                up = down = pltpu.roll(jnp.where(keep, two, one), LANES // 2, 1)
            else:
                up = pltpu.roll(two, size * bit, 1)
                down = pltpu.roll(one, LANES - size * bit, 1)
            blocks[i] = jnp.where(keep, one, up)
            blocks[j] = jnp.where(keep, down, two)
    return blocks


def compress_kernel(x_ref, squeeze_ref, out_ref, y_ref):
    squeeze = squeeze_ref[...]
    for r in range(0, ROWS, 2):
        pair = [jnp.concatenate(halves(x_ref[k]), axis=0) for k in (r, r + 1)]
        y = dot(squeeze, jnp.concatenate(pair, axis=1))
        y = y[:RANK] + y[RANK:]
        y_ref[r] = y[:, :LANES]
        y_ref[r + 1] = y[:, LANES:]
    for side in range(2):
        first = side * BLOCK_ROWS
        for c in range(0, HALF, 8):
            blocks = {}
            for r in range(BLOCK_ROWS):
                for half in range(2):
                    start = half * HALF + c
                    blocks[half * BLOCK_ROWS + r] = y_ref[first + r, start : start + 8, :]
            swap_groups(blocks, GROUP, (1, 2, 4, 8))
            for g in blocks:
                for j in range(g % 2, 3, 2):
                    at = j * HALF + c
                    out_ref[(g - j) % SECTORS + side, at : at + 8, :] = blocks[g]


def pack(ref, at, level):
    ref[0:8, :] = jnp.where(level < 4, at(2, 3), at(0, 3))
    ref[8:16, :] = jnp.where(level < 2, pltpu.roll(at(2, 2), 5, 0), at(0, 1))
    ref[16:24, :] = at(2, 1)
    ref[24:32, :] = jnp.where(level < 3, at(2, 2), at(0, 2))
    for d in range(1, 4):
        ref[24 + 8 * d : 32 + 8 * d, :] = at(1, d)


def to_source(ref, cells, high_ref, low_ref):
    cells_high, cells_low = halves(cells)
    count = cells.shape[0]
    both = jnp.concatenate([cells_high, cells_low], axis=0)
    for n in range(0, COEFS, 256):
        wide = dot(both, high_ref[:, n : n + 256])
        ref[:, n : n + 256] = (
            wide[:count] + wide[count:] + dot(cells_high, low_ref[:, n : n + 256])
        )


def border_kernel(p_ref, high_ref, low_ref, cross_ref, chip_ref, s_ref, inner_ref):
    outer, inner = [], []
    for j in range(3):
        block = p_ref[:, j * HALF : (j + 1) * HALF, :].reshape(SECTORS * HALF, LANES).T
        block = jnp.concatenate([block[:64], block[64:]], axis=1)
        outer += [block[:24], block[40:]]
        inner.append(block[24:40])
    inner_ref[...] = jnp.concatenate(inner, axis=0)
    to_source(s_ref, jnp.concatenate(outer, axis=0), high_ref, low_ref)
    core = lax.axis_index("azi") & 1
    level = lax.broadcasted_iota(jnp.int32, (8, COEFS), 0)

    def rows_from(end):
        def at(j, d):
            row = end * 3 + d - 1 + end * (4 - 2 * d)
            return s_ref[pl.ds(pl.multiple_of(j * 48 + row * 8, 8), 8), :]

        return at

    pack(cross_ref, rows_from(core), level)
    pack(chip_ref, rows_from(1 - core), level)


def unpack(load, distance, level):
    if distance == 3:
        both = load(0)
        return [both, load(48), both]
    if distance == 2:
        both = load(24)
        rest = pltpu.roll(load(8), 3, 0)
        return [both, load(40), jnp.where(level < 3, both, rest)]
    return [load(8), load(32), load(16)]


def factors():
    steps = []
    ratio = 1.0 / sigma
    for _ in range(SWEEPS - 1):
        following = 1.0 / (2.0 * sigma - ratio)
        steps.append((following * ratio, 2.0 * following / delta))
        ratio = following
    return steps


def vertical(center, level, cut):
    above = [pltpu.roll(x, 7, 0) for x in center]
    below = [pltpu.roll(x, 1, 0) for x in center]
    return [
        jnp.where(level == 7, above[1], above[0]) + below[0],
        jnp.where(level == 7, above[2] * cut, above[1])
        + jnp.where(level == 0, below[0], below[1]),
        above[2] + jnp.where(level == 0, below[1] * cut, below[2]),
    ]


def window_cut():
    last = (lax.axis_index("azi") >> 1) == BLOCKS - 1
    return jnp.where(jnp.full((8, LANES), last), 0.0, 1.0).astype(F32)


def main_kernel(
    count, s_ref, inner_ref, high_ref, low_ref, own_ref, inverse_ref, weight_ref, middle_ref
):
    to_source(middle_ref, inner_ref[...], high_ref, low_ref)
    shape = (8, LANES)
    level = lax.broadcasted_iota(jnp.int32, shape, 0)
    lane = lax.broadcasted_iota(jnp.int32, shape, 1)
    core = lax.axis_index("azi") & 1
    row_first = lax.axis_index("rad") * ROWS + core * BLOCK_ROWS
    cut = window_cut()

    for e in range(EXTENDED):
        row = jnp.full(shape, row_first + (e - 3), jnp.int32)
        inverse = 1.0 / (row.astype(F32) + 0.5)
        weight_ref[e, 0] = 1.0 + 0.5 * inverse
        weight_ref[e, 1] = 1.0 - 0.5 * inverse
        good = jnp.where((row >= 0) & (row < count * ROWS), 1.0, 0.0).astype(F32)
        for t in range(2):
            ratio = (lane + t * LANES).astype(F32) * inverse
            inverse_ref[t, e] = good / (4.0 + ratio * ratio)

    ratios = factors()

    @pl.loop(0, 4)
    def _(tile):
        lanes = pl.ds(pl.multiple_of(tile * LANES, LANES), LANES)
        table = tile % 2

        def source(r):
            if r in (3, 4):
                starts = [j * 16 + (r - 3) * 8 for j in range(3)]
                return [middle_ref[start : start + 8, lanes] for start in starts]
            starts = [j * 48 + (r if r < 3 else r - 2) * 8 for j in range(3)]
            return [s_ref[start : start + 8, lanes] for start in starts]

        given, scale, step = {}, {}, {}
        state = [{} for _ in range(SWEEPS)]
        for newest in range(3, EXTENDED + SWEEPS - 1):
            e = newest
            if e < 11:
                given[e] = source(e - 3)
                scale[e] = inverse_ref[table, e]
                step[e] = [g * scale[e] * (1.0 / theta) for g in given[e]]
                state[0][e] = step[e]
            for sweep in range(1, SWEEPS):
                e = newest - sweep
                reach = min(sweep, SWEEPS - 1 - sweep)
                if not 3 - reach <= e < 11 + reach:
                    continue
                keep, push = ratios[sweep - 1]
                steps, values = advance(
                    keep,
                    push,
                    state[sweep - 1],
                    given.get(e),
                    step.get(e),
                    e,
                    inverse_ref[table, e],
                    weight_ref[e, 0],
                    weight_ref[e, 1],
                    level,
                    cut,
                )
                step[e] = steps
                state[sweep][e] = values
            e = newest - (SWEEPS - 1)
            if 3 <= e < 11:
                x = state[SWEEPS - 1][e]
                at = (e - 3) * 16
                own_ref[at : at + 8, lanes] = jnp.where(level < 4, x[2], x[0])
                own_ref[at + 8 : at + 16, lanes] = x[1]


def advance(keep, push, old, given, step, e, scale, plus, minus, level, cut):
    center = old.get(e)
    near = vertical(center, level, cut) if center is not None else None
    steps, values = [], []
    for j in range(3):
        terms = []
        if given is not None:
            terms.append(given[j])
        if near is not None:
            terms.append(near[j])
        if e + 1 in old:
            terms.append(plus * old[e + 1][j])
        if e - 1 in old:
            terms.append(minus * old[e - 1][j])
        move = (push * scale) * sum(terms[1:], terms[0])
        if center is not None:
            move = move - push * center[j]
        if step is not None:
            move = move + keep * step[j]
        steps.append(move)
        values.append(move if center is None else center[j] + move)
    return steps, values


def edge_kernel(
    main_ref, inverse_ref, weight_ref, cross_ref, chip_ref, vh_ref, vl_ref, out_ref, own_ref
):
    level = lax.broadcasted_iota(jnp.int32, (8, LANES), 0)
    core = lax.axis_index("azi") & 1
    cut = window_cut()
    ratios = factors()
    own_ref[...] = main_ref[...]

    @pl.loop(0, 4, unroll=4)
    def _(tile):
        lanes = pl.ds(pl.multiple_of(tile * LANES, LANES), LANES)
        table = tile % 2
        for ref, turned in ((cross_ref, core), (chip_ref, 1 - core)):
            at = [t + turned * (EXTENDED - 1 - 2 * t) for t in range(6)]
            given = {
                t: unpack(lambda start: ref[start : start + 8, lanes], 3 - t, level)
                for t in range(3)
            }
            scale = [inverse_ref[table, e] for e in at]
            step = {t: [g * scale[t] * (1.0 / theta) for g in given[t]] for t in given}
            state = dict(step)
            for sweep in range(1, SWEEPS):
                keep, push = ratios[sweep - 1]
                fresh = {}
                for t in range(sweep, sweep + 3):
                    steps, fresh[t] = advance(
                        keep,
                        push,
                        state,
                        given.get(t),
                        step.get(t),
                        t,
                        scale[t],
                        weight_ref[at[t], turned],
                        weight_ref[at[t], 1 - turned],
                        level,
                        cut,
                    )
                    step[t] = steps
                state = fresh
            for t in range(3, 6):
                x = state[t]
                start = pl.multiple_of((at[t] - 3) * 16, 16)
                own_ref[pl.ds(start, 8), lanes] += jnp.where(level < 4, x[2], x[0])
                own_ref[pl.ds(start + 8, 8), lanes] += x[1]

    own_high, own_low = halves(own_ref[...])
    both = jnp.concatenate([own_high, own_low], axis=0)

    def across(a, b):
        return lax.dot_general(a, b, (((1,), (1,)), ((), ())), preferred_element_type=F32)

    step_rows = 384
    for m in range(0, SECTORS * RANK, step_rows):
        wide = across(vh_ref[m : m + step_rows, :], both)
        out_ref[m : m + step_rows, :] = (
            wide[:, :LANES]
            + wide[:, LANES:]
            + across(vl_ref[m : m + step_rows, :], own_high)
        )


def expand_kernel(q_ref, stretch_ref, out_hbm, y_ref, out_ref, sems):
    stretch = stretch_ref[...]
    first = lax.broadcasted_iota(jnp.int32, (8, LANES), 1) % (2 * GROUP) < 4
    rows = ROWS // CHUNKS
    copies = []
    for side in range(2):
        for c in range(0, RANK, 8):
            held = [q_ref[2 * b + side, c : c + 8, :] for b in range(BLOCKS)]
            blocks = {b: jnp.where(first, held[b - 1], held[b]) for b in range(BLOCKS)}
            swap_groups(blocks, 2 * GROUP, (1, 2, 4))
            for r in range(BLOCK_ROWS):
                y_ref[side * BLOCK_ROWS + r, c : c + 8, :] = blocks[r]
        for r in range(side * BLOCK_ROWS, (side + 1) * BLOCK_ROWS, 2):
            columns = []
            for k in range(2):
                high, low = halves(y_ref[r + k])
                columns.append(jnp.concatenate([high, low, high, low], axis=0))
            wide = dot(stretch, jnp.concatenate(columns, axis=1))
            out_ref[r] = wide[:, :LANES]
            out_ref[r + 1] = wide[:, LANES:]
            if (r + 2) % rows == 0:
                part = pl.ds(r + 2 - rows, rows)
                sem = sems.at[len(copies)]
                copies.append(pltpu.make_async_copy(out_ref.at[part], out_hbm.at[part], sem))
                copies[-1].start()
    for copy in copies:
        copy.wait()


VMEM = pl.BlockSpec(memory_space=pltpu.VMEM)
HBM = pl.BlockSpec(memory_space=pltpu.HBM)


def call(kernel, outs, in_specs, scratch, name, out_space=VMEM, **options):
    single = len(outs) == 1
    shapes = [jax.ShapeDtypeStruct(shape, F32) for shape in outs]
    return pl.pallas_call(
        kernel,
        out_shape=shapes[0] if single else shapes,
        in_specs=in_specs,
        out_specs=out_space if single else [out_space] * len(outs),
        scratch_shapes=scratch,
        compiler_params=pltpu.CompilerParams(vmem_limit_bytes=40 * 1024 * 1024),
        name=name,
        **options,
    )


def compress(density, squeeze, **options):
    return call(
        compress_kernel,
        [(SECTORS, 3 * HALF, LANES)],
        [VMEM] * 2,
        [pltpu.VMEM((ROWS, RANK, LANES), F32)],
        "compress",
        **options,
    )(density, squeeze)


def border_source(received, high, low, **options):
    return call(
        border_kernel,
        [(56, COEFS), (56, COEFS), (144, COEFS), (48, SECTORS * RANK)],
        [VMEM] * 3,
        [],
        "border_source",
        **options,
    )(received, high, low)


def solve_main(count, source, inner, high, low, **options):
    return call(
        functools.partial(main_kernel, count),
        [(LANES, COEFS), (2, EXTENDED, 8, LANES), (EXTENDED, 2, 8, LANES)],
        [VMEM] * 4,
        [pltpu.VMEM((48, COEFS), F32)],
        "solve_main",
        cost_estimate=pl.CostEstimate(
            flops=40_000_000, bytes_accessed=1_000_000, transcendentals=0
        ),
        **options,
    )(source, inner, high, low)


def solve_edge(main, inverse, weight, cross, chip, v_high, v_low, **options):
    return call(
        edge_kernel,
        [(SECTORS * RANK, LANES)],
        [VMEM] * 7,
        [pltpu.VMEM((LANES, COEFS), F32)],
        "solve_edge",
        **options,
    )(main, inverse, weight, cross, chip, v_high, v_low)


def expand(received, stretch, **options):
    return call(
        expand_kernel,
        [(ROWS, SECTOR, DEPTH)],
        [VMEM] * 2,
        [
            pltpu.VMEM((ROWS, RANK, LANES), F32),
            pltpu.VMEM((ROWS, SECTOR, DEPTH), F32),
            pltpu.SemaphoreType.DMA((CHUNKS,)),
        ],
        "expand",
        out_space=HBM,
        **options,
    )(received, stretch)


def per_device(density):
    squeeze, forward, inverse, stretch = (
        jax.tree.map(jnp.asarray, item) for item in tables()
    )
    count = lax.axis_size("rad")
    held = lax.reduce_precision(density, 8, 23)
    outgoing = compress(held, squeeze)
    received = lax.all_to_all(outgoing, "azi", 0, 0)
    cross, chip, source, inner = border_source(received, *forward)
    swaps = []
    for device in range(1, (count - 1) * SECTORS, 2):
        swaps += [(device, device + SECTORS - 1), (device + SECTORS - 1, device)]
    cross = lax.ppermute(cross, ("rad", "azi"), swaps)
    chip = lax.ppermute(chip, "azi", [(i, i ^ 1) for i in range(SECTORS)])
    main, scales, weights = solve_main(count, source, inner, *forward)
    solved = solve_edge(main, scales, weights, cross, chip, *inverse)
    received = lax.all_to_all(solved.reshape(SECTORS, RANK, LANES), "azi", 0, 0)
    return expand(received, stretch)


def solution(mesh):
    spec = P("rad", "azi", None)
    return jax.shard_map(
        per_device, mesh=mesh, in_specs=(spec,), out_specs=spec, check_vma=False
    )
```

```python
import functools
import math

import jax
import jax.numpy as jnp
import numpy as np
from jax import lax
from jax.experimental import pallas as pl
from jax.experimental.pallas import tpu as pltpu
from jax.sharding import PartitionSpec as P

NPHI = 2048
MODES = 256
SWEEPS = 4
SECTORS = 16
SECTOR = NPHI // SECTORS
COEFS = 2 * MODES
RANK = 48
ROWS = 16
DEPTH = 128
GROUP = 8
LANES = 128
HALF = RANK // 2
BLOCKS = 8
BLOCK_ROWS = 8
EXTENDED = BLOCK_ROWS + 6
CELLS = 3 * GROUP * BLOCK_ROWS
CHUNKS = 4

low_bound = 0.1
high_bound = 2.0
theta = 0.5 * (high_bound + low_bound)
delta = 0.5 * (high_bound - low_bound)
sigma = theta / delta
four_pi = 4.0 * math.pi

BF = jnp.bfloat16
F32 = jnp.float32


def split_table(table):
    high = table.astype(np.float32).astype(BF)
    low = (table - high.astype(np.float64)).astype(np.float32).astype(BF)
    return high, low


@functools.cache
def tables():
    modes = np.arange(MODES)
    angle = 2.0 * np.pi * ((np.arange(SECTOR)[:, None] * modes[None, :]) % NPHI) / NPHI
    first = np.concatenate([np.cos(angle), np.sin(angle)], axis=1)
    left, _, _ = np.linalg.svd(first, full_matrices=False)
    left = left[:, :RANK]
    cores = []
    for sector in range(SECTORS):
        cells = sector * SECTOR + np.arange(SECTOR)
        angle = 2.0 * np.pi * ((cells[:, None] * modes[None, :]) % NPHI) / NPHI
        cores.append(left.T @ np.concatenate([np.cos(angle), np.sin(angle)], axis=1))
    core = np.concatenate(cores, axis=0)
    weight = np.where(np.tile(modes, 2) == 0, 1.0, 2.0)
    left_high, left_low = split_table(left)
    ordered = core.reshape(SECTORS, 2, HALF, COEFS).transpose(1, 0, 2, 3)
    forward = split_table(ordered.reshape(SECTORS * RANK, COEFS) * (-four_pi / NPHI))
    inverse = split_table(core * weight[None, :])
    squeeze = np.concatenate(
        [
            np.concatenate([left_high.T, left_high.T], axis=1),
            np.concatenate([left_low.T, left_low.T], axis=1),
        ],
        axis=0,
    )
    stretch = np.concatenate([left_high, left_high, left_low, left_low], axis=1)
    return squeeze, forward, inverse, stretch


def halves(value):
    high = value.astype(BF)
    low = (value - high.astype(F32)).astype(BF)
    return high, low


def dot(a, b):
    return jnp.dot(a, b, preferred_element_type=F32)


def swap_groups(blocks, size, bits):
    group = lax.broadcasted_iota(jnp.int32, next(iter(blocks.values())).shape, 1) // size
    for bit in bits:
        keep = (group & bit) == 0
        for i in list(blocks):
            if i & bit:
                continue
            j = i | bit
            one, two = blocks[i], blocks[j]
            if 2 * size * bit == LANES:
                up = down = pltpu.roll(jnp.where(keep, two, one), LANES // 2, 1)
            else:
                up = pltpu.roll(two, size * bit, 1)
                down = pltpu.roll(one, LANES - size * bit, 1)
            blocks[i] = jnp.where(keep, one, up)
            blocks[j] = jnp.where(keep, down, two)
    return blocks


def compress_kernel(x_ref, squeeze_ref, out_ref, y_ref):
    squeeze = squeeze_ref[...]
    for r in range(0, ROWS, 2):
        pair = [jnp.concatenate(halves(x_ref[k]), axis=0) for k in (r, r + 1)]
        y = dot(squeeze, jnp.concatenate(pair, axis=1))
        y = y[:RANK] + y[RANK:]
        y_ref[r] = y[:, :LANES]
        y_ref[r + 1] = y[:, LANES:]
    for side in range(2):
        first = side * BLOCK_ROWS
        for c in range(0, HALF, 8):
            blocks = {}
            for r in range(BLOCK_ROWS):
                for half in range(2):
                    start = half * HALF + c
                    blocks[half * BLOCK_ROWS + r] = y_ref[first + r, start : start + 8, :]
            swap_groups(blocks, GROUP, (1, 2, 4, 8))
            for g in blocks:
                for j in range(g % 2, 3, 2):
                    at = j * HALF + c
                    out_ref[(g - j) % SECTORS + side, at : at + 8, :] = blocks[g]


def pack(ref, at, level):
    ref[0:8, :] = jnp.where(level < 4, at(2, 3), at(0, 3))
    ref[8:16, :] = jnp.where(level < 2, pltpu.roll(at(2, 2), 5, 0), at(0, 1))
    ref[16:24, :] = at(2, 1)
    ref[24:32, :] = jnp.where(level < 3, at(2, 2), at(0, 2))
    for d in range(1, 4):
        ref[24 + 8 * d : 32 + 8 * d, :] = at(1, d)


def to_source(ref, cells, high_ref, low_ref):
    cells_high, cells_low = halves(cells)
    count = cells.shape[0]
    both = jnp.concatenate([cells_high, cells_low], axis=0)
    for n in range(0, COEFS, 256):
        wide = dot(both, high_ref[:, n : n + 256])
        ref[:, n : n + 256] = (
            wide[:count] + wide[count:] + dot(cells_high, low_ref[:, n : n + 256])
        )


def border_kernel(p_ref, high_ref, low_ref, cross_ref, chip_ref, s_ref, inner_ref):
    outer, inner = [], []
    for j in range(3):
        block = p_ref[:, j * HALF : (j + 1) * HALF, :].reshape(SECTORS * HALF, LANES).T
        block = jnp.concatenate([block[:64], block[64:]], axis=1)
        outer += [block[:24], block[40:]]
        inner.append(block[24:40])
    inner_ref[...] = jnp.concatenate(inner, axis=0)
    to_source(s_ref, jnp.concatenate(outer, axis=0), high_ref, low_ref)
    core = lax.axis_index("azi") & 1
    level = lax.broadcasted_iota(jnp.int32, (8, COEFS), 0)

    def rows_from(end):
        def at(j, d):
            row = end * 3 + d - 1 + end * (4 - 2 * d)
            return s_ref[pl.ds(pl.multiple_of(j * 48 + row * 8, 8), 8), :]

        return at

    pack(cross_ref, rows_from(core), level)
    pack(chip_ref, rows_from(1 - core), level)


def unpack(load, distance, level):
    if distance == 3:
        both = load(0)
        return [both, load(48), both]
    if distance == 2:
        both = load(24)
        rest = pltpu.roll(load(8), 3, 0)
        return [both, load(40), jnp.where(level < 3, both, rest)]
    return [load(8), load(32), load(16)]


def factors():
    steps = []
    ratio = 1.0 / sigma
    for _ in range(SWEEPS - 1):
        following = 1.0 / (2.0 * sigma - ratio)
        steps.append((following * ratio, 2.0 * following / delta))
        ratio = following
    return steps


def vertical(center, level, cut):
    above = [pltpu.roll(x, 7, 0) for x in center]
    below = [pltpu.roll(x, 1, 0) for x in center]
    return [
        jnp.where(level == 7, above[1], above[0]) + below[0],
        jnp.where(level == 7, above[2] * cut, above[1])
        + jnp.where(level == 0, below[0], below[1]),
        above[2] + jnp.where(level == 0, below[1] * cut, below[2]),
    ]


def window_cut():
    last = (lax.axis_index("azi") >> 1) == BLOCKS - 1
    return jnp.where(jnp.full((8, LANES), last), 0.0, 1.0).astype(F32)


def main_kernel(
    count, s_ref, inner_ref, high_ref, low_ref, own_ref, inverse_ref, weight_ref, middle_ref
):
    to_source(middle_ref, inner_ref[...], high_ref, low_ref)
    shape = (8, LANES)
    level = lax.broadcasted_iota(jnp.int32, shape, 0)
    lane = lax.broadcasted_iota(jnp.int32, shape, 1)
    core = lax.axis_index("azi") & 1
    row_first = lax.axis_index("rad") * ROWS + core * BLOCK_ROWS
    cut = window_cut()

    for e in range(EXTENDED):
        row = jnp.full(shape, row_first + (e - 3), jnp.int32)
        inverse = 1.0 / (row.astype(F32) + 0.5)
        weight_ref[e, 0] = 1.0 + 0.5 * inverse
        weight_ref[e, 1] = 1.0 - 0.5 * inverse
        good = jnp.where((row >= 0) & (row < count * ROWS), 1.0, 0.0).astype(F32)
        for t in range(2):
            ratio = (lane + t * LANES).astype(F32) * inverse
            inverse_ref[t, e] = good / (4.0 + ratio * ratio)

    ratios = factors()

    @pl.loop(0, 4)
    def _(tile):
        lanes = pl.ds(pl.multiple_of(tile * LANES, LANES), LANES)
        table = tile % 2

        def source(r):
            if r in (3, 4):
                starts = [j * 16 + (r - 3) * 8 for j in range(3)]
                return [middle_ref[start : start + 8, lanes] for start in starts]
            starts = [j * 48 + (r if r < 3 else r - 2) * 8 for j in range(3)]
            return [s_ref[start : start + 8, lanes] for start in starts]

        given, scale, step = {}, {}, {}
        state = [{} for _ in range(SWEEPS)]
        for newest in range(3, EXTENDED + SWEEPS - 1):
            e = newest
            if e < 11:
                given[e] = source(e - 3)
                scale[e] = inverse_ref[table, e]
                step[e] = [g * scale[e] * (1.0 / theta) for g in given[e]]
                state[0][e] = step[e]
            for sweep in range(1, SWEEPS):
                e = newest - sweep
                reach = min(sweep, SWEEPS - 1 - sweep)
                if not 3 - reach <= e < 11 + reach:
                    continue
                keep, push = ratios[sweep - 1]
                steps, values = advance(
                    keep,
                    push,
                    state[sweep - 1],
                    given.get(e),
                    step.get(e),
                    e,
                    inverse_ref[table, e],
                    weight_ref[e, 0],
                    weight_ref[e, 1],
                    level,
                    cut,
                )
                step[e] = steps
                state[sweep][e] = values
            e = newest - (SWEEPS - 1)
            if 3 <= e < 11:
                x = state[SWEEPS - 1][e]
                at = (e - 3) * 16
                own_ref[at : at + 8, lanes] = jnp.where(level < 4, x[2], x[0])
                own_ref[at + 8 : at + 16, lanes] = x[1]


def advance(keep, push, old, given, step, e, scale, plus, minus, level, cut):
    center = old.get(e)
    near = vertical(center, level, cut) if center is not None else None
    steps, values = [], []
    for j in range(3):
        terms = []
        if given is not None:
            terms.append(given[j])
        if near is not None:
            terms.append(near[j])
        if e + 1 in old:
            terms.append(plus * old[e + 1][j])
        if e - 1 in old:
            terms.append(minus * old[e - 1][j])
        move = (push * scale) * sum(terms[1:], terms[0])
        if center is not None:
            move = move - push * center[j]
        if step is not None:
            move = move + keep * step[j]
        steps.append(move)
        values.append(move if center is None else center[j] + move)
    return steps, values


def add_reach(main_ref, inverse_ref, weight_ref, edge_ref, side, own_ref):
    level = lax.broadcasted_iota(jnp.int32, (8, LANES), 0)
    cut = window_cut()
    ratios = factors()
    own_ref[...] = main_ref[...]

    @pl.loop(0, 4, unroll=4)
    def _(tile):
        lanes = pl.ds(pl.multiple_of(tile * LANES, LANES), LANES)
        table = tile % 2
        for ref, turned in ((edge_ref, side),):
            at = [t + turned * (EXTENDED - 1 - 2 * t) for t in range(6)]
            given = {
                t: unpack(lambda start: ref[start : start + 8, lanes], 3 - t, level)
                for t in range(3)
            }
            scale = [inverse_ref[table, e] for e in at]
            step = {t: [g * scale[t] * (1.0 / theta) for g in given[t]] for t in given}
            state = dict(step)
            for sweep in range(1, SWEEPS):
                keep, push = ratios[sweep - 1]
                fresh = {}
                for t in range(sweep, sweep + 3):
                    steps, fresh[t] = advance(
                        keep,
                        push,
                        state,
                        given.get(t),
                        step.get(t),
                        t,
                        scale[t],
                        weight_ref[at[t], turned],
                        weight_ref[at[t], 1 - turned],
                        level,
                        cut,
                    )
                    step[t] = steps
                state = fresh
            for t in range(3, 6):
                x = state[t]
                start = pl.multiple_of((at[t] - 3) * 16, 16)
                own_ref[pl.ds(start, 8), lanes] += jnp.where(level < 4, x[2], x[0])
                own_ref[pl.ds(start + 8, 8), lanes] += x[1]


def chip_kernel(main_ref, inverse_ref, weight_ref, chip_ref, own_ref):
    core = lax.axis_index("azi") & 1
    add_reach(main_ref, inverse_ref, weight_ref, chip_ref, 1 - core, own_ref)


def edge_kernel(main_ref, inverse_ref, weight_ref, cross_ref, vh_ref, vl_ref, out_ref, own_ref):
    core = lax.axis_index("azi") & 1
    add_reach(main_ref, inverse_ref, weight_ref, cross_ref, core, own_ref)

    own_high, own_low = halves(own_ref[...])
    both = jnp.concatenate([own_high, own_low], axis=0)

    def across(a, b):
        return lax.dot_general(a, b, (((1,), (1,)), ((), ())), preferred_element_type=F32)

    step_rows = 384
    for m in range(0, SECTORS * RANK, step_rows):
        wide = across(vh_ref[m : m + step_rows, :], both)
        out_ref[m : m + step_rows, :] = (
            wide[:, :LANES]
            + wide[:, LANES:]
            + across(vl_ref[m : m + step_rows, :], own_high)
        )


def expand_kernel(q_ref, stretch_ref, out_hbm, y_ref, out_ref, sems):
    stretch = stretch_ref[...]
    first = lax.broadcasted_iota(jnp.int32, (8, LANES), 1) % (2 * GROUP) < 4
    rows = ROWS // CHUNKS
    copies = []
    for side in range(2):
        for c in range(0, RANK, 8):
            held = [q_ref[2 * b + side, c : c + 8, :] for b in range(BLOCKS)]
            blocks = {b: jnp.where(first, held[b - 1], held[b]) for b in range(BLOCKS)}
            swap_groups(blocks, 2 * GROUP, (1, 2, 4))
            for r in range(BLOCK_ROWS):
                y_ref[side * BLOCK_ROWS + r, c : c + 8, :] = blocks[r]
        for r in range(side * BLOCK_ROWS, (side + 1) * BLOCK_ROWS, 2):
            columns = []
            for k in range(2):
                high, low = halves(y_ref[r + k])
                columns.append(jnp.concatenate([high, low, high, low], axis=0))
            wide = dot(stretch, jnp.concatenate(columns, axis=1))
            out_ref[r] = wide[:, :LANES]
            out_ref[r + 1] = wide[:, LANES:]
            if (r + 2) % rows == 0:
                part = pl.ds(r + 2 - rows, rows)
                sem = sems.at[len(copies)]
                copies.append(pltpu.make_async_copy(out_ref.at[part], out_hbm.at[part], sem))
                copies[-1].start()
    for copy in copies:
        copy.wait()


VMEM = pl.BlockSpec(memory_space=pltpu.VMEM)
HBM = pl.BlockSpec(memory_space=pltpu.HBM)


def call(kernel, outs, in_specs, scratch, name, out_space=VMEM, **options):
    single = len(outs) == 1
    shapes = [jax.ShapeDtypeStruct(shape, F32) for shape in outs]
    return pl.pallas_call(
        kernel,
        out_shape=shapes[0] if single else shapes,
        in_specs=in_specs,
        out_specs=out_space if single else [out_space] * len(outs),
        scratch_shapes=scratch,
        compiler_params=pltpu.CompilerParams(vmem_limit_bytes=40 * 1024 * 1024),
        name=name,
        **options,
    )


def compress(density, squeeze, **options):
    return call(
        compress_kernel,
        [(SECTORS, 3 * HALF, LANES)],
        [VMEM] * 2,
        [pltpu.VMEM((ROWS, RANK, LANES), F32)],
        "compress",
        **options,
    )(density, squeeze)


def border_source(received, high, low, **options):
    return call(
        border_kernel,
        [(56, COEFS), (56, COEFS), (144, COEFS), (48, SECTORS * RANK)],
        [VMEM] * 3,
        [],
        "border_source",
        **options,
    )(received, high, low)


def solve_main(count, source, inner, high, low, **options):
    return call(
        functools.partial(main_kernel, count),
        [(LANES, COEFS), (2, EXTENDED, 8, LANES), (EXTENDED, 2, 8, LANES)],
        [VMEM] * 4,
        [pltpu.VMEM((48, COEFS), F32)],
        "solve_main",
        cost_estimate=pl.CostEstimate(
            flops=40_000_000, bytes_accessed=1_000_000, transcendentals=0
        ),
        **options,
    )(source, inner, high, low)


def solve_chip(main, inverse, weight, chip, **options):
    return call(
        chip_kernel,
        [(LANES, COEFS)],
        [VMEM] * 4,
        [],
        "solve_chip",
        **options,
    )(main, inverse, weight, chip)


def solve_edge(main, inverse, weight, cross, v_high, v_low, **options):
    return call(
        edge_kernel,
        [(SECTORS * RANK, LANES)],
        [VMEM] * 6,
        [pltpu.VMEM((LANES, COEFS), F32)],
        "solve_edge",
        **options,
    )(main, inverse, weight, cross, v_high, v_low)


def expand(received, stretch, **options):
    return call(
        expand_kernel,
        [(ROWS, SECTOR, DEPTH)],
        [VMEM] * 2,
        [
            pltpu.VMEM((ROWS, RANK, LANES), F32),
            pltpu.VMEM((ROWS, SECTOR, DEPTH), F32),
            pltpu.SemaphoreType.DMA((CHUNKS,)),
        ],
        "expand",
        out_space=HBM,
        **options,
    )(received, stretch)


def per_device(density):
    squeeze, forward, inverse, stretch = (
        jax.tree.map(jnp.asarray, item) for item in tables()
    )
    count = lax.axis_size("rad")
    held = lax.reduce_precision(density, 8, 23)
    outgoing = compress(held, squeeze)
    received = lax.all_to_all(outgoing, "azi", 0, 0)
    cross, chip, source, inner = border_source(received, *forward)
    swaps = []
    for device in range(1, (count - 1) * SECTORS, 2):
        swaps += [(device, device + SECTORS - 1), (device + SECTORS - 1, device)]
    cross = lax.ppermute(cross, ("rad", "azi"), swaps)
    chip = lax.ppermute(chip, "azi", [(i, i ^ 1) for i in range(SECTORS)])
    main, scales, weights = solve_main(count, source, inner, *forward)
    main = solve_chip(main, scales, weights, chip)
    solved = solve_edge(main, scales, weights, cross, *inverse)
    received = lax.all_to_all(solved.reshape(SECTORS, RANK, LANES), "azi", 0, 0)
    return expand(received, stretch)


def solution(mesh):
    spec = P("rad", "azi", None)
    return jax.shard_map(
        per_device, mesh=mesh, in_specs=(spec,), out_specs=spec, check_vma=False
    )
```

```python
import functools
import math

import jax
import jax.numpy as jnp
import numpy as np
from jax import lax
from jax.experimental import pallas as pl
from jax.experimental.pallas import tpu as pltpu
from jax.sharding import PartitionSpec as P

NPHI = 2048
MODES = 256
SWEEPS = 4
SECTORS = 16
SECTOR = NPHI // SECTORS
COEFS = 2 * MODES
RANK = 48
ROWS = 16
DEPTH = 128
GROUP = 8
LANES = 128
HALF = RANK // 2
BLOCKS = 8
BLOCK_ROWS = 8
EXTENDED = BLOCK_ROWS + 6
CELLS = 3 * GROUP * BLOCK_ROWS
CHUNKS = 4

low_bound = 0.1
high_bound = 2.0
theta = 0.5 * (high_bound + low_bound)
delta = 0.5 * (high_bound - low_bound)
sigma = theta / delta
four_pi = 4.0 * math.pi

BF = jnp.bfloat16
F32 = jnp.float32


def split_table(table):
    high = table.astype(np.float32).astype(BF)
    low = (table - high.astype(np.float64)).astype(np.float32).astype(BF)
    return high, low


@functools.cache
def tables():
    modes = np.arange(MODES)
    angle = 2.0 * np.pi * ((np.arange(SECTOR)[:, None] * modes[None, :]) % NPHI) / NPHI
    first = np.concatenate([np.cos(angle), np.sin(angle)], axis=1)
    left, _, _ = np.linalg.svd(first, full_matrices=False)
    left = left[:, :RANK]
    cores = []
    for sector in range(SECTORS):
        cells = sector * SECTOR + np.arange(SECTOR)
        angle = 2.0 * np.pi * ((cells[:, None] * modes[None, :]) % NPHI) / NPHI
        cores.append(left.T @ np.concatenate([np.cos(angle), np.sin(angle)], axis=1))
    core = np.concatenate(cores, axis=0)
    weight = np.where(np.tile(modes, 2) == 0, 1.0, 2.0)
    left_high, left_low = split_table(left)
    ordered = core.reshape(SECTORS, 2, HALF, COEFS).transpose(1, 0, 2, 3)
    forward = split_table(ordered.reshape(SECTORS * RANK, COEFS) * (-four_pi / NPHI))
    inverse = split_table(core * weight[None, :])
    squeeze = np.concatenate(
        [
            np.concatenate([left_high.T, left_high.T], axis=1),
            np.concatenate([left_low.T, left_low.T], axis=1),
        ],
        axis=0,
    )
    stretch = np.concatenate([left_high, left_high, left_low], axis=1)
    return squeeze, forward, inverse, stretch


def halves(value):
    high = value.astype(BF)
    low = (value - high.astype(F32)).astype(BF)
    return high, low


def dot(a, b):
    return jnp.dot(a, b, preferred_element_type=F32)


def swap_groups(blocks, size, bits):
    group = lax.broadcasted_iota(jnp.int32, next(iter(blocks.values())).shape, 1) // size
    for bit in bits:
        keep = (group & bit) == 0
        for i in list(blocks):
            if i & bit:
                continue
            j = i | bit
            one, two = blocks[i], blocks[j]
            if 2 * size * bit == LANES:
                up = down = pltpu.roll(jnp.where(keep, two, one), LANES // 2, 1)
            else:
                up = pltpu.roll(two, size * bit, 1)
                down = pltpu.roll(one, LANES - size * bit, 1)
            blocks[i] = jnp.where(keep, one, up)
            blocks[j] = jnp.where(keep, down, two)
    return blocks


def compress_kernel(x_ref, squeeze_ref, out_ref, y_ref):
    squeeze = squeeze_ref[...]
    for r in range(0, ROWS, 2):
        pair = [jnp.concatenate(halves(x_ref[k]), axis=0) for k in (r, r + 1)]
        y = dot(squeeze, jnp.concatenate(pair, axis=1))
        y = y[:RANK] + y[RANK:]
        y_ref[r] = y[:, :LANES]
        y_ref[r + 1] = y[:, LANES:]
    for side in range(2):
        first = side * BLOCK_ROWS
        for c in range(0, HALF, 8):
            blocks = {}
            for r in range(BLOCK_ROWS):
                for half in range(2):
                    start = half * HALF + c
                    blocks[half * BLOCK_ROWS + r] = y_ref[first + r, start : start + 8, :]
            swap_groups(blocks, GROUP, (1, 2, 4, 8))
            for g in blocks:
                for j in range(g % 2, 3, 2):
                    at = j * HALF + c
                    out_ref[(g - j) % SECTORS + side, at : at + 8, :] = blocks[g]


def pack(ref, at, level):
    ref[0:8, :] = jnp.where(level < 4, at(2, 3), at(0, 3))
    ref[8:16, :] = jnp.where(level < 2, pltpu.roll(at(2, 2), 5, 0), at(0, 1))
    ref[16:24, :] = at(2, 1)
    ref[24:32, :] = jnp.where(level < 3, at(2, 2), at(0, 2))
    for d in range(1, 4):
        ref[24 + 8 * d : 32 + 8 * d, :] = at(1, d)


def to_source(ref, cells, high_ref, low_ref):
    cells_high, cells_low = halves(cells)
    count = cells.shape[0]
    both = jnp.concatenate([cells_high, cells_low], axis=0)
    for n in range(0, COEFS, 256):
        wide = dot(both, high_ref[:, n : n + 256])
        ref[:, n : n + 256] = (
            wide[:count] + wide[count:] + dot(cells_high, low_ref[:, n : n + 256])
        )


def border_kernel(p_ref, high_ref, low_ref, cross_ref, chip_ref, s_ref, inner_ref):
    outer, inner = [], []
    for j in range(3):
        block = p_ref[:, j * HALF : (j + 1) * HALF, :].reshape(SECTORS * HALF, LANES).T
        block = jnp.concatenate([block[:64], block[64:]], axis=1)
        outer += [block[:24], block[40:]]
        inner.append(block[24:40])
    inner_ref[...] = jnp.concatenate(inner, axis=0)
    to_source(s_ref, jnp.concatenate(outer, axis=0), high_ref, low_ref)
    core = lax.axis_index("azi") & 1
    level = lax.broadcasted_iota(jnp.int32, (8, COEFS), 0)

    def rows_from(end):
        def at(j, d):
            row = end * 3 + d - 1 + end * (4 - 2 * d)
            return s_ref[pl.ds(pl.multiple_of(j * 48 + row * 8, 8), 8), :]

        return at

    pack(cross_ref, rows_from(core), level)
    pack(chip_ref, rows_from(1 - core), level)


def unpack(load, distance, level):
    if distance == 3:
        both = load(0)
        return [both, load(48), both]
    if distance == 2:
        both = load(24)
        rest = pltpu.roll(load(8), 3, 0)
        return [both, load(40), jnp.where(level < 3, both, rest)]
    return [load(8), load(32), load(16)]


def factors():
    steps = []
    ratio = 1.0 / sigma
    for _ in range(SWEEPS - 1):
        following = 1.0 / (2.0 * sigma - ratio)
        steps.append((following * ratio, 2.0 * following / delta))
        ratio = following
    return steps


def vertical(center, level, cut):
    above = [pltpu.roll(x, 7, 0) for x in center]
    below = [pltpu.roll(x, 1, 0) for x in center]
    return [
        jnp.where(level == 7, above[1], above[0]) + below[0],
        jnp.where(level == 7, above[2] * cut, above[1])
        + jnp.where(level == 0, below[0], below[1]),
        above[2] + jnp.where(level == 0, below[1] * cut, below[2]),
    ]


def window_cut():
    last = (lax.axis_index("azi") >> 1) == BLOCKS - 1
    return jnp.where(jnp.full((8, LANES), last), 0.0, 1.0).astype(F32)


def main_kernel(
    count, s_ref, inner_ref, high_ref, low_ref, own_ref, inverse_ref, weight_ref, middle_ref
):
    to_source(middle_ref, inner_ref[...], high_ref, low_ref)
    shape = (8, LANES)
    level = lax.broadcasted_iota(jnp.int32, shape, 0)
    lane = lax.broadcasted_iota(jnp.int32, shape, 1)
    core = lax.axis_index("azi") & 1
    row_first = lax.axis_index("rad") * ROWS + core * BLOCK_ROWS
    cut = window_cut()

    for e in range(EXTENDED):
        row = jnp.full(shape, row_first + (e - 3), jnp.int32)
        inverse = 1.0 / (row.astype(F32) + 0.5)
        weight_ref[e, 0] = 1.0 + 0.5 * inverse
        weight_ref[e, 1] = 1.0 - 0.5 * inverse
        good = jnp.where((row >= 0) & (row < count * ROWS), 1.0, 0.0).astype(F32)
        for t in range(2):
            ratio = (lane + t * LANES).astype(F32) * inverse
            inverse_ref[t, e] = good / (4.0 + ratio * ratio)

    ratios = factors()

    @pl.loop(0, 4)
    def _(tile):
        lanes = pl.ds(pl.multiple_of(tile * LANES, LANES), LANES)
        table = tile % 2

        def source(r):
            if r in (3, 4):
                starts = [j * 16 + (r - 3) * 8 for j in range(3)]
                return [middle_ref[start : start + 8, lanes] for start in starts]
            starts = [j * 48 + (r if r < 3 else r - 2) * 8 for j in range(3)]
            return [s_ref[start : start + 8, lanes] for start in starts]

        given, scale, step = {}, {}, {}
        state = [{} for _ in range(SWEEPS)]
        for newest in range(3, EXTENDED + SWEEPS - 1):
            e = newest
            if e < 11:
                given[e] = source(e - 3)
                scale[e] = inverse_ref[table, e]
                step[e] = [g * scale[e] * (1.0 / theta) for g in given[e]]
                state[0][e] = step[e]
            for sweep in range(1, SWEEPS):
                e = newest - sweep
                reach = min(sweep, SWEEPS - 1 - sweep)
                if not 3 - reach <= e < 11 + reach:
                    continue
                keep, push = ratios[sweep - 1]
                steps, values = advance(
                    keep,
                    push,
                    state[sweep - 1],
                    given.get(e),
                    step.get(e),
                    e,
                    inverse_ref[table, e],
                    weight_ref[e, 0],
                    weight_ref[e, 1],
                    level,
                    cut,
                )
                step[e] = steps
                state[sweep][e] = values
            e = newest - (SWEEPS - 1)
            if 3 <= e < 11:
                x = state[SWEEPS - 1][e]
                at = (e - 3) * 16
                own_ref[at : at + 8, lanes] = jnp.where(level < 4, x[2], x[0])
                own_ref[at + 8 : at + 16, lanes] = x[1]


def advance(keep, push, old, given, step, e, scale, plus, minus, level, cut):
    center = old.get(e)
    near = vertical(center, level, cut) if center is not None else None
    steps, values = [], []
    for j in range(3):
        terms = []
        if given is not None:
            terms.append(given[j])
        if near is not None:
            terms.append(near[j])
        if e + 1 in old:
            terms.append(plus * old[e + 1][j])
        if e - 1 in old:
            terms.append(minus * old[e - 1][j])
        move = (push * scale) * sum(terms[1:], terms[0])
        if center is not None:
            move = move - push * center[j]
        if step is not None:
            move = move + keep * step[j]
        steps.append(move)
        values.append(move if center is None else center[j] + move)
    return steps, values


def edge_kernel(
    main_ref, inverse_ref, weight_ref, cross_ref, chip_ref, vh_ref, vl_ref, out_ref, own_ref
):
    level = lax.broadcasted_iota(jnp.int32, (8, LANES), 0)
    core = lax.axis_index("azi") & 1
    cut = window_cut()
    ratios = factors()
    own_ref[...] = main_ref[...]

    @pl.loop(0, 4, unroll=4)
    def _(tile):
        lanes = pl.ds(pl.multiple_of(tile * LANES, LANES), LANES)
        table = tile % 2
        for ref, turned in ((cross_ref, core), (chip_ref, 1 - core)):
            at = [t + turned * (EXTENDED - 1 - 2 * t) for t in range(6)]
            given = {
                t: unpack(lambda start: ref[start : start + 8, lanes], 3 - t, level)
                for t in range(3)
            }
            scale = [inverse_ref[table, e] for e in at]
            step = {t: [g * scale[t] * (1.0 / theta) for g in given[t]] for t in given}
            state = dict(step)
            for sweep in range(1, SWEEPS):
                keep, push = ratios[sweep - 1]
                fresh = {}
                for t in range(sweep, sweep + 3):
                    steps, fresh[t] = advance(
                        keep,
                        push,
                        state,
                        given.get(t),
                        step.get(t),
                        t,
                        scale[t],
                        weight_ref[at[t], turned],
                        weight_ref[at[t], 1 - turned],
                        level,
                        cut,
                    )
                    step[t] = steps
                state = fresh
            for t in range(3, 6):
                x = state[t]
                start = pl.multiple_of((at[t] - 3) * 16, 16)
                own_ref[pl.ds(start, 8), lanes] += jnp.where(level < 4, x[2], x[0])
                own_ref[pl.ds(start + 8, 8), lanes] += x[1]

    own_high, own_low = halves(own_ref[...])
    both = jnp.concatenate([own_high, own_low], axis=0)

    def across(a, b):
        return lax.dot_general(a, b, (((1,), (1,)), ((), ())), preferred_element_type=F32)

    step_rows = 384
    for m in range(0, SECTORS * RANK, step_rows):
        wide = across(vh_ref[m : m + step_rows, :], both)
        out_ref[m : m + step_rows, :] = (
            wide[:, :LANES]
            + wide[:, LANES:]
            + across(vl_ref[m : m + step_rows, :], own_high)
        )


def expand_kernel(q_ref, stretch_ref, out_hbm, y_ref, out_ref, sems):
    stretch = stretch_ref[...]
    first = lax.broadcasted_iota(jnp.int32, (8, LANES), 1) % (2 * GROUP) < 4
    rows = ROWS // CHUNKS
    copies = []
    for side in range(2):
        for c in range(0, RANK, 8):
            held = [q_ref[2 * b + side, c : c + 8, :] for b in range(BLOCKS)]
            blocks = {b: jnp.where(first, held[b - 1], held[b]) for b in range(BLOCKS)}
            swap_groups(blocks, 2 * GROUP, (1, 2, 4))
            for r in range(BLOCK_ROWS):
                y_ref[side * BLOCK_ROWS + r, c : c + 8, :] = blocks[r]
        for r in range(side * BLOCK_ROWS, (side + 1) * BLOCK_ROWS, 2):
            columns = []
            for k in range(2):
                high, low = halves(y_ref[r + k])
                columns.append(jnp.concatenate([high, low, high], axis=0))
            wide = dot(stretch, jnp.concatenate(columns, axis=1))
            out_ref[r] = wide[:, :LANES]
            out_ref[r + 1] = wide[:, LANES:]
            if (r + 2) % rows == 0:
                part = pl.ds(r + 2 - rows, rows)
                sem = sems.at[len(copies)]
                copies.append(pltpu.make_async_copy(out_ref.at[part], out_hbm.at[part], sem))
                copies[-1].start()
    for copy in copies:
        copy.wait()


VMEM = pl.BlockSpec(memory_space=pltpu.VMEM)
HBM = pl.BlockSpec(memory_space=pltpu.HBM)


def call(kernel, outs, in_specs, scratch, name, out_space=VMEM, **options):
    single = len(outs) == 1
    shapes = [jax.ShapeDtypeStruct(shape, F32) for shape in outs]
    return pl.pallas_call(
        kernel,
        out_shape=shapes[0] if single else shapes,
        in_specs=in_specs,
        out_specs=out_space if single else [out_space] * len(outs),
        scratch_shapes=scratch,
        compiler_params=pltpu.CompilerParams(vmem_limit_bytes=40 * 1024 * 1024),
        name=name,
        **options,
    )


def compress(density, squeeze, **options):
    return call(
        compress_kernel,
        [(SECTORS, 3 * HALF, LANES)],
        [VMEM] * 2,
        [pltpu.VMEM((ROWS, RANK, LANES), F32)],
        "compress",
        **options,
    )(density, squeeze)


def border_source(received, high, low, **options):
    return call(
        border_kernel,
        [(56, COEFS), (56, COEFS), (144, COEFS), (48, SECTORS * RANK)],
        [VMEM] * 3,
        [],
        "border_source",
        **options,
    )(received, high, low)


def solve_main(count, source, inner, high, low, **options):
    return call(
        functools.partial(main_kernel, count),
        [(LANES, COEFS), (2, EXTENDED, 8, LANES), (EXTENDED, 2, 8, LANES)],
        [VMEM] * 4,
        [pltpu.VMEM((48, COEFS), F32)],
        "solve_main",
        cost_estimate=pl.CostEstimate(
            flops=40_000_000, bytes_accessed=1_000_000, transcendentals=0
        ),
        **options,
    )(source, inner, high, low)


def solve_edge(main, inverse, weight, cross, chip, v_high, v_low, **options):
    return call(
        edge_kernel,
        [(SECTORS * RANK, LANES)],
        [VMEM] * 7,
        [pltpu.VMEM((LANES, COEFS), F32)],
        "solve_edge",
        **options,
    )(main, inverse, weight, cross, chip, v_high, v_low)


def expand(received, stretch, **options):
    return call(
        expand_kernel,
        [(ROWS, SECTOR, DEPTH)],
        [VMEM] * 2,
        [
            pltpu.VMEM((ROWS, RANK, LANES), F32),
            pltpu.VMEM((ROWS, SECTOR, DEPTH), F32),
            pltpu.SemaphoreType.DMA((CHUNKS,)),
        ],
        "expand",
        out_space=HBM,
        **options,
    )(received, stretch)


def per_device(density):
    squeeze, forward, inverse, stretch = (
        jax.tree.map(jnp.asarray, item) for item in tables()
    )
    count = lax.axis_size("rad")
    held = lax.reduce_precision(density, 8, 23)
    outgoing = compress(held, squeeze)
    received = lax.all_to_all(outgoing, "azi", 0, 0)
    cross, chip, source, inner = border_source(received, *forward)
    swaps = []
    for device in range(1, (count - 1) * SECTORS, 2):
        swaps += [(device, device + SECTORS - 1), (device + SECTORS - 1, device)]
    cross = lax.ppermute(cross, ("rad", "azi"), swaps)
    chip = lax.ppermute(chip, "azi", [(i, i ^ 1) for i in range(SECTORS)])
    main, scales, weights = solve_main(count, source, inner, *forward)
    solved = solve_edge(main, scales, weights, cross, chip, *inverse)
    received = lax.all_to_all(solved.reshape(SECTORS, RANK, LANES), "azi", 0, 0)
    return expand(received, stretch)


def solution(mesh):
    spec = P("rad", "azi", None)
    return jax.shard_map(
        per_device, mesh=mesh, in_specs=(spec,), out_specs=spec, check_vma=False
    )
```

```python
import functools
import math

import jax
import jax.numpy as jnp
import numpy as np
from jax import lax
from jax.experimental import pallas as pl
from jax.experimental.pallas import tpu as pltpu
from jax.sharding import PartitionSpec as P

NPHI = 2048
MODES = 256
SWEEPS = 4
SECTORS = 16
SECTOR = NPHI // SECTORS
COEFS = 2 * MODES
RANK = 48
ROWS = 16
DEPTH = 128
GROUP = 8
LANES = 128
HALF = RANK // 2
BLOCKS = 8
BLOCK_ROWS = 8
EXTENDED = BLOCK_ROWS + 6
CELLS = 3 * GROUP * BLOCK_ROWS
CHUNKS = 4

low_bound = 0.1
high_bound = 2.0
theta = 0.5 * (high_bound + low_bound)
delta = 0.5 * (high_bound - low_bound)
sigma = theta / delta
four_pi = 4.0 * math.pi

BF = jnp.bfloat16
F32 = jnp.float32


def split_table(table):
    high = table.astype(np.float32).astype(BF)
    low = (table - high.astype(np.float64)).astype(np.float32).astype(BF)
    return high, low


@functools.cache
def tables():
    modes = np.arange(MODES)
    angle = 2.0 * np.pi * ((np.arange(SECTOR)[:, None] * modes[None, :]) % NPHI) / NPHI
    first = np.concatenate([np.cos(angle), np.sin(angle)], axis=1)
    left, _, _ = np.linalg.svd(first, full_matrices=False)
    left = left[:, :RANK]
    cores = []
    for sector in range(SECTORS):
        cells = sector * SECTOR + np.arange(SECTOR)
        angle = 2.0 * np.pi * ((cells[:, None] * modes[None, :]) % NPHI) / NPHI
        cores.append(left.T @ np.concatenate([np.cos(angle), np.sin(angle)], axis=1))
    core = np.concatenate(cores, axis=0)
    weight = np.where(np.tile(modes, 2) == 0, 1.0, 2.0)
    left_high, left_low = split_table(left)
    ordered = core.reshape(SECTORS, 2, HALF, COEFS).transpose(1, 0, 2, 3)
    forward = split_table(ordered.reshape(SECTORS * RANK, COEFS) * (-four_pi / NPHI))
    inverse = split_table(core * weight[None, :])
    squeeze = np.concatenate(
        [
            np.concatenate([left_high.T, left_high.T], axis=1),
            np.concatenate([left_low.T, left_low.T], axis=1),
        ],
        axis=0,
    )
    stretch = np.concatenate([left_high, left_high, left_low, left_low], axis=1)
    return squeeze, forward, inverse, stretch


def halves(value):
    high = value.astype(BF)
    low = (value - high.astype(F32)).astype(BF)
    return high, low


def dot(a, b):
    return jnp.dot(a, b, preferred_element_type=F32)


def swap_groups(blocks, size, bits):
    group = lax.broadcasted_iota(jnp.int32, next(iter(blocks.values())).shape, 1) // size
    for bit in bits:
        keep = (group & bit) == 0
        for i in list(blocks):
            if i & bit:
                continue
            j = i | bit
            one, two = blocks[i], blocks[j]
            if 2 * size * bit == LANES:
                up = down = pltpu.roll(jnp.where(keep, two, one), LANES // 2, 1)
            else:
                up = pltpu.roll(two, size * bit, 1)
                down = pltpu.roll(one, LANES - size * bit, 1)
            blocks[i] = jnp.where(keep, one, up)
            blocks[j] = jnp.where(keep, down, two)
    return blocks


def compress_kernel(x_ref, squeeze_ref, out_ref, y_ref):
    squeeze = squeeze_ref[...]
    for r in range(0, ROWS, 2):
        pair = [jnp.concatenate(halves(x_ref[k]), axis=0) for k in (r, r + 1)]
        y = dot(squeeze, jnp.concatenate(pair, axis=1))
        y = y[:RANK] + y[RANK:]
        y_ref[r] = y[:, :LANES]
        y_ref[r + 1] = y[:, LANES:]
    for side in range(2):
        first = side * BLOCK_ROWS
        for c in range(0, HALF, 8):
            blocks = {}
            for r in range(BLOCK_ROWS):
                for half in range(2):
                    start = half * HALF + c
                    blocks[half * BLOCK_ROWS + r] = y_ref[first + r, start : start + 8, :]
            swap_groups(blocks, GROUP, (1, 2, 4, 8))
            for g in blocks:
                for j in range(g % 2, 3, 2):
                    at = j * HALF + c
                    out_ref[(g - j) % SECTORS + side, at : at + 8, :] = blocks[g]


def pack(ref, at, level):
    ref[0:8, :] = jnp.where(level < 4, at(2, 3), at(0, 3))
    ref[8:16, :] = jnp.where(level < 2, pltpu.roll(at(2, 2), 5, 0), at(0, 1))
    ref[16:24, :] = at(2, 1)
    ref[24:32, :] = jnp.where(level < 3, at(2, 2), at(0, 2))
    for d in range(1, 4):
        ref[24 + 8 * d : 32 + 8 * d, :] = at(1, d)


def to_source(ref, cells, high_ref, low_ref):
    cells_high, cells_low = halves(cells)
    count = cells.shape[0]
    both = jnp.concatenate([cells_high, cells_low], axis=0)
    for n in range(0, COEFS, 256):
        wide = dot(both, high_ref[:, n : n + 256])
        ref[:, n : n + 256] = (
            wide[:count] + wide[count:] + dot(cells_high, low_ref[:, n : n + 256])
        )


def border_kernel(p_ref, high_ref, low_ref, cross_ref, chip_ref, s_ref, inner_ref):
    outer, inner = [], []
    for j in range(3):
        block = p_ref[:, j * HALF : (j + 1) * HALF, :].reshape(SECTORS * HALF, LANES).T
        block = jnp.concatenate([block[:64], block[64:]], axis=1)
        outer += [block[:24], block[40:]]
        inner.append(block[24:40])
    inner_ref[...] = jnp.concatenate(inner, axis=0)
    to_source(s_ref, jnp.concatenate(outer, axis=0), high_ref, low_ref)
    core = lax.axis_index("azi") & 1
    level = lax.broadcasted_iota(jnp.int32, (8, COEFS), 0)

    def rows_from(end):
        def at(j, d):
            row = end * 3 + d - 1 + end * (4 - 2 * d)
            return s_ref[pl.ds(pl.multiple_of(j * 48 + row * 8, 8), 8), :]

        return at

    pack(cross_ref, rows_from(core), level)
    pack(chip_ref, rows_from(1 - core), level)


def unpack(load, distance, level):
    if distance == 3:
        both = load(0)
        return [both, load(48), both]
    if distance == 2:
        both = load(24)
        rest = pltpu.roll(load(8), 3, 0)
        return [both, load(40), jnp.where(level < 3, both, rest)]
    return [load(8), load(32), load(16)]


def factors():
    steps = []
    ratio = 1.0 / sigma
    for _ in range(SWEEPS - 1):
        following = 1.0 / (2.0 * sigma - ratio)
        steps.append((following * ratio, 2.0 * following / delta))
        ratio = following
    return steps


def vertical(center, level, cut):
    above = [pltpu.roll(x, 7, 0) for x in center]
    below = [pltpu.roll(x, 1, 0) for x in center]
    return [
        jnp.where(level == 7, above[1], above[0]) + below[0],
        jnp.where(level == 7, above[2] * cut, above[1])
        + jnp.where(level == 0, below[0], below[1]),
        above[2] + jnp.where(level == 0, below[1] * cut, below[2]),
    ]


def window_cut():
    last = (lax.axis_index("azi") >> 1) == BLOCKS - 1
    return jnp.where(jnp.full((8, LANES), last), 0.0, 1.0).astype(F32)


def main_kernel(
    count, s_ref, inner_ref, high_ref, low_ref, own_ref, inverse_ref, weight_ref, middle_ref
):
    to_source(middle_ref, inner_ref[...], high_ref, low_ref)
    shape = (8, LANES)
    level = lax.broadcasted_iota(jnp.int32, shape, 0)
    lane = lax.broadcasted_iota(jnp.int32, shape, 1)
    core = lax.axis_index("azi") & 1
    row_first = lax.axis_index("rad") * ROWS + core * BLOCK_ROWS
    cut = window_cut()

    for e in range(EXTENDED):
        row = jnp.full(shape, row_first + (e - 3), jnp.int32)
        inverse = 1.0 / (row.astype(F32) + 0.5)
        weight_ref[e, 0] = 1.0 + 0.5 * inverse
        weight_ref[e, 1] = 1.0 - 0.5 * inverse
        good = jnp.where((row >= 0) & (row < count * ROWS), 1.0, 0.0).astype(F32)
        for t in range(2):
            ratio = (lane + t * LANES).astype(F32) * inverse
            inverse_ref[t, e] = good / (4.0 + ratio * ratio)

    ratios = factors()

    @pl.loop(0, 4)
    def _(tile):
        lanes = pl.ds(pl.multiple_of(tile * LANES, LANES), LANES)
        table = tile % 2

        def source(r):
            if r in (3, 4):
                starts = [j * 16 + (r - 3) * 8 for j in range(3)]
                return [middle_ref[start : start + 8, lanes] for start in starts]
            starts = [j * 48 + (r if r < 3 else r - 2) * 8 for j in range(3)]
            return [s_ref[start : start + 8, lanes] for start in starts]

        given, scale, step = {}, {}, {}
        state = [{} for _ in range(SWEEPS)]
        for newest in range(3, EXTENDED + SWEEPS - 1):
            e = newest
            if e < 11:
                given[e] = source(e - 3)
                scale[e] = inverse_ref[table, e]
                step[e] = [g * scale[e] * (1.0 / theta) for g in given[e]]
                state[0][e] = step[e]
            for sweep in range(1, SWEEPS):
                e = newest - sweep
                reach = min(sweep, SWEEPS - 1 - sweep)
                if not 3 - reach <= e < 11 + reach:
                    continue
                keep, push = ratios[sweep - 1]
                steps, values = advance(
                    keep,
                    push,
                    state[sweep - 1],
                    given.get(e),
                    step.get(e),
                    e,
                    inverse_ref[table, e],
                    weight_ref[e, 0],
                    weight_ref[e, 1],
                    level,
                    cut,
                )
                step[e] = steps
                state[sweep][e] = values
            e = newest - (SWEEPS - 1)
            if 3 <= e < 11:
                x = state[SWEEPS - 1][e]
                at = (e - 3) * 16
                own_ref[at : at + 8, lanes] = jnp.where(level < 4, x[2], x[0])
                own_ref[at + 8 : at + 16, lanes] = x[1]


def advance(keep, push, old, given, step, e, scale, plus, minus, level, cut):
    center = old.get(e)
    near = vertical(center, level, cut) if center is not None else None
    steps, values = [], []
    for j in range(3):
        terms = []
        if given is not None:
            terms.append(given[j])
        if near is not None:
            terms.append(near[j])
        if e + 1 in old:
            terms.append(plus * old[e + 1][j])
        if e - 1 in old:
            terms.append(minus * old[e - 1][j])
        move = (push * scale) * sum(terms[1:], terms[0])
        if center is not None:
            move = move - push * center[j]
        if step is not None:
            move = move + keep * step[j]
        steps.append(move)
        values.append(move if center is None else center[j] + move)
    return steps, values


def edge_kernel(
    main_ref, inverse_ref, weight_ref, cross_ref, chip_ref, vh_ref, vl_ref, out_ref, own_ref
):
    level = lax.broadcasted_iota(jnp.int32, (8, LANES), 0)
    core = lax.axis_index("azi") & 1
    cut = window_cut()
    ratios = factors()
    own_ref[48:80, :] = main_ref[48:80, :]

    @pl.loop(0, 4, unroll=4)
    def _(tile):
        lanes = pl.ds(pl.multiple_of(tile * LANES, LANES), LANES)
        table = tile % 2
        for ref, turned in ((cross_ref, core), (chip_ref, 1 - core)):
            at = [t + turned * (EXTENDED - 1 - 2 * t) for t in range(6)]
            given = {
                t: unpack(lambda start: ref[start : start + 8, lanes], 3 - t, level)
                for t in range(3)
            }
            scale = [inverse_ref[table, e] for e in at]
            step = {t: [g * scale[t] * (1.0 / theta) for g in given[t]] for t in given}
            state = dict(step)
            for sweep in range(1, SWEEPS):
                keep, push = ratios[sweep - 1]
                fresh = {}
                for t in range(sweep, sweep + 3):
                    steps, fresh[t] = advance(
                        keep,
                        push,
                        state,
                        given.get(t),
                        step.get(t),
                        t,
                        scale[t],
                        weight_ref[at[t], turned],
                        weight_ref[at[t], 1 - turned],
                        level,
                        cut,
                    )
                    step[t] = steps
                state = fresh
            for t in range(3, 6):
                x = state[t]
                start = pl.multiple_of((at[t] - 3) * 16, 16)
                added = jnp.where(level < 4, x[2], x[0])
                own_ref[pl.ds(start, 8), lanes] = main_ref[pl.ds(start, 8), lanes] + added
                own_ref[pl.ds(start + 8, 8), lanes] = main_ref[pl.ds(start + 8, 8), lanes] + x[1]

    own_high, own_low = halves(own_ref[...])
    both = jnp.concatenate([own_high, own_low], axis=0)

    def across(a, b):
        return lax.dot_general(a, b, (((1,), (1,)), ((), ())), preferred_element_type=F32)

    step_rows = 384
    for m in range(0, SECTORS * RANK, step_rows):
        wide = across(vh_ref[m : m + step_rows, :], both)
        out_ref[m : m + step_rows, :] = (
            wide[:, :LANES]
            + wide[:, LANES:]
            + across(vl_ref[m : m + step_rows, :], own_high)
        )


def expand_kernel(q_ref, stretch_ref, out_hbm, y_ref, out_ref, sems):
    stretch = stretch_ref[...]
    first = lax.broadcasted_iota(jnp.int32, (8, LANES), 1) % (2 * GROUP) < 4
    rows = ROWS // CHUNKS
    copies = []
    for side in range(2):
        for c in range(0, RANK, 8):
            held = [q_ref[2 * b + side, c : c + 8, :] for b in range(BLOCKS)]
            blocks = {b: jnp.where(first, held[b - 1], held[b]) for b in range(BLOCKS)}
            swap_groups(blocks, 2 * GROUP, (1, 2, 4))
            for r in range(BLOCK_ROWS):
                y_ref[side * BLOCK_ROWS + r, c : c + 8, :] = blocks[r]
        for r in range(side * BLOCK_ROWS, (side + 1) * BLOCK_ROWS, 2):
            columns = []
            for k in range(2):
                high, low = halves(y_ref[r + k])
                columns.append(jnp.concatenate([high, low, high, low], axis=0))
            wide = dot(stretch, jnp.concatenate(columns, axis=1))
            out_ref[r] = wide[:, :LANES]
            out_ref[r + 1] = wide[:, LANES:]
            if (r + 2) % rows == 0:
                part = pl.ds(r + 2 - rows, rows)
                sem = sems.at[len(copies)]
                copies.append(pltpu.make_async_copy(out_ref.at[part], out_hbm.at[part], sem))
                copies[-1].start()
    for copy in copies:
        copy.wait()


VMEM = pl.BlockSpec(memory_space=pltpu.VMEM)
HBM = pl.BlockSpec(memory_space=pltpu.HBM)


def call(kernel, outs, in_specs, scratch, name, out_space=VMEM, **options):
    single = len(outs) == 1
    shapes = [jax.ShapeDtypeStruct(shape, F32) for shape in outs]
    return pl.pallas_call(
        kernel,
        out_shape=shapes[0] if single else shapes,
        in_specs=in_specs,
        out_specs=out_space if single else [out_space] * len(outs),
        scratch_shapes=scratch,
        compiler_params=pltpu.CompilerParams(vmem_limit_bytes=40 * 1024 * 1024),
        name=name,
        **options,
    )


def compress(density, squeeze, **options):
    return call(
        compress_kernel,
        [(SECTORS, 3 * HALF, LANES)],
        [VMEM] * 2,
        [pltpu.VMEM((ROWS, RANK, LANES), F32)],
        "compress",
        **options,
    )(density, squeeze)


def border_source(received, high, low, **options):
    return call(
        border_kernel,
        [(56, COEFS), (56, COEFS), (144, COEFS), (48, SECTORS * RANK)],
        [VMEM] * 3,
        [],
        "border_source",
        **options,
    )(received, high, low)


def solve_main(count, source, inner, high, low, **options):
    return call(
        functools.partial(main_kernel, count),
        [(LANES, COEFS), (2, EXTENDED, 8, LANES), (EXTENDED, 2, 8, LANES)],
        [VMEM] * 4,
        [pltpu.VMEM((48, COEFS), F32)],
        "solve_main",
        cost_estimate=pl.CostEstimate(
            flops=40_000_000, bytes_accessed=1_000_000, transcendentals=0
        ),
        **options,
    )(source, inner, high, low)


def solve_edge(main, inverse, weight, cross, chip, v_high, v_low, **options):
    return call(
        edge_kernel,
        [(SECTORS * RANK, LANES)],
        [VMEM] * 7,
        [pltpu.VMEM((LANES, COEFS), F32)],
        "solve_edge",
        **options,
    )(main, inverse, weight, cross, chip, v_high, v_low)


def expand(received, stretch, **options):
    return call(
        expand_kernel,
        [(ROWS, SECTOR, DEPTH)],
        [VMEM] * 2,
        [
            pltpu.VMEM((ROWS, RANK, LANES), F32),
            pltpu.VMEM((ROWS, SECTOR, DEPTH), F32),
            pltpu.SemaphoreType.DMA((CHUNKS,)),
        ],
        "expand",
        out_space=HBM,
        **options,
    )(received, stretch)


def per_device(density):
    squeeze, forward, inverse, stretch = (
        jax.tree.map(jnp.asarray, item) for item in tables()
    )
    count = lax.axis_size("rad")
    held = lax.reduce_precision(density, 8, 23)
    outgoing = compress(held, squeeze)
    received = lax.all_to_all(outgoing, "azi", 0, 0)
    cross, chip, source, inner = border_source(received, *forward)
    swaps = []
    for device in range(1, (count - 1) * SECTORS, 2):
        swaps += [(device, device + SECTORS - 1), (device + SECTORS - 1, device)]
    cross = lax.ppermute(cross, ("rad", "azi"), swaps)
    chip = lax.ppermute(chip, "azi", [(i, i ^ 1) for i in range(SECTORS)])
    main, scales, weights = solve_main(count, source, inner, *forward)
    solved = solve_edge(main, scales, weights, cross, chip, *inverse)
    received = lax.all_to_all(solved.reshape(SECTORS, RANK, LANES), "azi", 0, 0)
    return expand(received, stretch)


def solution(mesh):
    spec = P("rad", "azi", None)
    return jax.shard_map(
        per_device, mesh=mesh, in_specs=(spec,), out_specs=spec, check_vma=False
    )
```
